256 devices in a mesh: dp: 32 (over z, x_hi, core), fsdp: 8 (over y, x_lo).
Axes of the slice: x: 4 (x_hi: 2, x_lo: 2; x = x_hi * 2 + x_lo), y: 4, z: 8, core: 2. Of those that a mesh axis runs over, the one named last changes fastest.
Arguments:
- hidden: bfloat16 [256, 2, 128, 2560], P(('dp', 'fsdp')), may hold values from -6 to 6
- targets: bfloat16 [256, 2, 128, 2560], P(('dp', 'fsdp')), may hold values from -6 to 6
- lengths: int32 [256, 2], P(('dp', 'fsdp')), may hold values from 32 to 128
- prompt_group_index: int32 [256, 1], P(('dp', 'fsdp')), may hold values from 0 to 15
- input_norm_gain: float32 [2560], replicated, may hold values from 0.1 to 1.9
- frozen_weight: bfloat16 [2560, 3584], P('fsdp'), may hold values from -0.125 to 0.125
- adapter_down: bfloat16 [2560, 128], replicated, may hold values from -0.125 to 0.125
- adapter_up: bfloat16 [3072, 64], replicated, may hold values from -0.75 to 0.75
Outputs:
- pair_loss: float32 [256], P(('dp', 'fsdp'))
- grad_a: float32 [2560, 128], P('fsdp')
- grad_b: float32 [3072, 64], P('fsdp')
The draws below stay inside these ranges and needn't reach their ends.
All inputs are finite; a program needn't handle non-finite values.
Results may differ from the reference program's by a relative error of at most 0.038.
Values may be sent and summed in bfloat16 or wider, within the bound.
A program may use at most 128 MiB of HBM per device.

```python
import jax
import jax.numpy as jnp
from jax import lax

MODEL_FEATURES = 2560
QUERY_HEADS = 20
KEY_VALUE_HEADS = 4
HEAD_SIZE = 128
ADAPTER_RANK = 64
GROUPS = 16
L = 128
PAIRS = 256


def place_ends(array, stream_key, least, high):
    longest = array.shape.index(max(array.shape))
    spots = []
    for shift in (0, 1):
        where = [jax.random.randint(jax.random.fold_in(stream_key, axis), (), 0, length) for axis, length in enumerate(array.shape)]
        where[longest] = (where[longest] + shift) % array.shape[longest]
        spots.append(tuple(where))
    return array.at[spots[0]].set(least).at[spots[1]].set(high)


def block_levels(rng, shape, pieces, low, largest):
    level = 1.0
    for axis_at, blocks in pieces:
        draws = jax.random.uniform(jax.random.fold_in(jax.random.fold_in(rng, 6), axis_at), (blocks,), jnp.float32, low / len(pieces), largest / len(pieces))
        level = level * jnp.repeat(jnp.exp(draws), shape[axis_at] // blocks).reshape((-1,) + (1,) * (len(shape) - 1 - axis_at))
    return level


def picks_of(rng, rows, count, top, lift):
    order = jax.random.permutation(jax.random.fold_in(rng, 1), count)
    pull = order
    for power in range(3):
        pull = pull * pull // count
    pull = pull * lift // count
    chance = jax.random.randint(jax.random.fold_in(rng, 2), (rows, count), 0, 4096) + pull
    fixed_rows = jax.random.permutation(jax.random.fold_in(rng, 3), rows)[jnp.arange(count) % rows]
    chance = jnp.where(jnp.arange(rows)[:, None] == fixed_rows[None, :], 1 << 14, chance)
    score = chance * count + jnp.arange(count)
    return lax.top_k(score.astype(jnp.int32), top)[1].astype(jnp.int32)


def centred(key, dims, scale, reach, shards=(), kind=jnp.bfloat16):
    result = scale * jax.random.normal(key, dims, jnp.float32)
    if shards:
        result = result * block_levels(key, dims, shards, -0.22, 0.18)
    return jnp.clip(result, -reach, reach).astype(kind)


def setup_inputs(seed: int = 0) -> dict:
    key_list = jax.random.split(jax.random.key(seed), 9)
    return {
        "hidden": centred(key_list[0], (PAIRS, 2, L, MODEL_FEATURES), 1.0, 6.0, ((0, 256),)),
        "targets": centred(key_list[1], (PAIRS, 2, L, QUERY_HEADS * HEAD_SIZE), 1.0, 6.0, ((0, 256),)),
        "lengths": place_ends(jax.random.randint(key_list[2], (PAIRS, 2), L // 4, L + 1), jax.random.fold_in(key_list[2], 1), L // 4, L).astype(jnp.int32),
        "prompt_group_index": picks_of(key_list[3], PAIRS, GROUPS, 1, 512),
        "input_norm_gain": jnp.clip(1.0 + 0.18 * jax.random.normal(key_list[4], (MODEL_FEATURES,), jnp.float32), 0.1, 1.9),
        "frozen_weight": centred(key_list[5], (MODEL_FEATURES, (QUERY_HEADS + 2 * KEY_VALUE_HEADS) * HEAD_SIZE), MODEL_FEATURES ** -0.5, 0.125, ((0, 8),)),
        "adapter_down": centred(key_list[6], (MODEL_FEATURES, 2 * ADAPTER_RANK), MODEL_FEATURES ** -0.5, 0.125),
        "adapter_up": centred(key_list[7], ((QUERY_HEADS + KEY_VALUE_HEADS) * HEAD_SIZE, ADAPTER_RANK), ADAPTER_RANK ** -0.5, 0.75),
    }


EPS = 1e-05
BETA = 0.1
ADAPT_SCALE = 0.5

def normed_rows(rows, gain):
    values = rows.astype(jnp.float32)
    power = lax.optimization_barrier(jnp.mean(values * values, -1, keepdims=True))
    return (values * lax.rsqrt(power + EPS) * gain).astype(jnp.bfloat16)

def seq_scores(query, keys, values, target, lengths):
    seqs, slots, qwidth = query.shape
    kvheads = keys.shape[-1] // HEAD_SIZE
    groups = qwidth // HEAD_SIZE // kvheads
    q_heads = query.reshape(seqs, slots, kvheads, groups, HEAD_SIZE).astype(jnp.float32)
    k_heads = keys.reshape(seqs, slots, kvheads, HEAD_SIZE).astype(jnp.float32)
    v_heads = values.reshape(seqs, slots, kvheads, HEAD_SIZE).astype(jnp.float32)
    scores = jnp.einsum('nqhgd,nshd->nhgqs', q_heads, k_heads) * HEAD_SIZE ** (-0.5)
    places = jnp.arange(slots, dtype=jnp.int32)
    causal = places[None, :] <= places[:, None]
    inside = places[None, None, :] < lengths[:, None, None]
    allowed = (causal[None, :, :] & inside)[:, None, None, :, :]
    expo = jnp.where(allowed, jnp.exp(scores), jnp.float32(0.0))
    probs = (expo / lax.optimization_barrier(jnp.sum(expo, -1, keepdims=True))).astype(jnp.bfloat16)
    attended = jnp.einsum('nhgqs,nshd->nqhgd', probs.astype(jnp.float32), v_heads)
    attended = attended.astype(jnp.bfloat16).reshape(seqs, slots, qwidth)
    token = lax.optimization_barrier(jnp.sum(attended.astype(jnp.float32) * target.astype(jnp.float32), -1)) * qwidth ** (-0.5)
    valid = places[None, :] < lengths[:, None]
    return lax.optimization_barrier(jnp.sum(jnp.where(valid, token, jnp.float32(0.0)), -1))

def split_base(base_offset):
    qwidth = QUERY_HEADS * HEAD_SIZE
    key_value_width = KEY_VALUE_HEADS * HEAD_SIZE
    return (base_offset[:, :qwidth], base_offset[:, qwidth:qwidth + key_value_width], base_offset[:, qwidth + key_value_width:])

def contract_rows(left, right):
    return lax.dot_general(left, right, (((0,), (0,)), ((), ())), preferred_element_type=jnp.float32)

def pairwise_compute(normalized_input, base_offset, target, lengths, weight, first, second):
    seqs = target.shape[0]
    qwidth = QUERY_HEADS * HEAD_SIZE
    base_q, base_k, base_v = split_base(base_offset)
    keys = base_k.astype(jnp.bfloat16).reshape(seqs, -1, base_k.shape[-1])
    ref_scores = seq_scores(base_q.astype(jnp.bfloat16).reshape(seqs, -1, qwidth), keys, base_v.astype(jnp.bfloat16).reshape(seqs, -1, base_v.shape[-1]), target, lengths)
    lowrank = jnp.dot(normalized_input, first, preferred_element_type=jnp.float32).astype(jnp.bfloat16)
    up_q = second[:qwidth]
    up_v = second[qwidth:]
    upper_q = jnp.dot(lowrank[:, :ADAPTER_RANK], up_q.T, preferred_element_type=jnp.float32)
    upper_v = jnp.dot(lowrank[:, ADAPTER_RANK:], up_v.T, preferred_element_type=jnp.float32)
    query = (base_q + ADAPT_SCALE * upper_q).astype(jnp.bfloat16)
    values = (base_v + ADAPT_SCALE * upper_v).astype(jnp.bfloat16)

    def scored(qrows, vrows):
        return seq_scores(qrows.reshape(seqs, -1, qwidth), keys, vrows.reshape(seqs, -1, vrows.shape[-1]), target, lengths)
    pol_scores, pullback = jax.vjp(scored, query, values)
    pol_pairs = pol_scores.reshape(-1, 2)
    ref_pairs = ref_scores.reshape(-1, 2)
    margin = BETA * (pol_pairs[:, 0] - ref_pairs[:, 0] - (pol_pairs[:, 1] - ref_pairs[:, 1]))
    objective_loss = jax.nn.softplus(-margin)
    slope = -jax.nn.sigmoid(-margin) * weight * BETA
    cotangent = jnp.stack([slope, -slope], -1).reshape(-1)
    d_query, d_values = pullback(cotangent)
    grad_bq = ADAPT_SCALE * contract_rows(d_query, lowrank[:, :ADAPTER_RANK])
    grad_bv = ADAPT_SCALE * contract_rows(d_values, lowrank[:, ADAPTER_RANK:])
    low_q = jnp.dot(d_query, up_q, preferred_element_type=jnp.float32)
    low_v = jnp.dot(d_values, up_v, preferred_element_type=jnp.float32)
    d_low = (ADAPT_SCALE * jnp.concatenate([low_q, low_v], -1)).astype(jnp.bfloat16)
    gradient_leading = contract_rows(normalized_input, d_low)
    gradient_trailing = jnp.concatenate([grad_bq, grad_bv], 0)
    return (objective_loss, gradient_leading, gradient_trailing)

def reference(hidden, targets, lengths, prompt_group_index, input_norm_gain, frozen_weight, adapter_down, adapter_up):
    member = jax.nn.one_hot(prompt_group_index[:, 0], GROUPS, dtype=jnp.float32)
    counts = lax.optimization_barrier(jnp.sum(member, 0))
    weight_list = 1.0 / (GROUPS * lax.optimization_barrier(jnp.sum(member * counts[None, :], -1)))

    def step(carry, item):
        pair_rows, pairwise_target, pairwise_lengths, pairwise_weight = item
        normalized_input = normed_rows(pair_rows.reshape(-1, pair_rows.shape[-1]), input_norm_gain)
        base_offset = jnp.dot(normalized_input, frozen_weight, preferred_element_type=jnp.float32)
        objective_loss, gradient_leading, gradient_trailing = pairwise_compute(normalized_input, base_offset, pairwise_target, pairwise_lengths, pairwise_weight[None], adapter_down, adapter_up)
        return ((carry[0] + gradient_leading, carry[1] + gradient_trailing), objective_loss[0])
    start_offset = (jnp.zeros(adapter_down.shape, jnp.float32), jnp.zeros(adapter_up.shape, jnp.float32))
    totals, losses = lax.scan(step, start_offset, (hidden, targets, lengths, weight_list))
    return (losses, totals[0], totals[1])
```

```python
import jax
import jax.numpy as jnp
from jax import lax
from jax.experimental import pallas as pl
from jax.experimental.pallas import tpu as pltpu
from jax.sharding import PartitionSpec as P

MODEL = 2560
HEAD = 128
RANK = 64
GROUPS = 16
EPS = 1e-05
BETA = 0.1
ADAPT_SCALE = 0.5

NZ, NX, NY = 8, 4, 4
SHARD = 320
HALF = 160
UNITS = 14
AHEAD0, AHEAD1, AHEAD2 = 4, 2, 1

MESH = pl.DeviceIdType.MESH
F32 = jnp.float32
BF16 = jnp.bfloat16


def mm(a, b):
    return lax.dot_general(a, b, (((1,), (0,)), ((), ())), preferred_element_type=F32)


def mm_nt(a, b):
    return lax.dot_general(a, b, (((1,), (1,)), ((), ())), preferred_element_type=F32)


def kernel(
    len_ref,
    grp_ref,
    gain_ref,
    hid_hbm,
    tgt_hbm,
    w_hbm,
    down_hbm,
    up_hbm,
    loss_ref,
    ga_ref,
    gb_ref,
    wbuf,
    hbuf,
    normed,
    normed_t,
    tbuf,
    down,
    up,
    lowq,
    lowv,
    low_t,
    kbuf,
    vpol,
    vref,
    mask,
    sacc,
    dvacc,
    dq_all,
    xsum,
    xrecv,
    meta,
    cnt,
    cbuf_y,
    cbuf_x,
    cbuf_z,
    red,
    red1,
    red2,
    ry,
    rx,
    rz,
    fin,
    wsem,
    lsem,
    y_send,
    y_recv,
    x_send,
    x_recv,
    d_send,
    d_recv,
    q_send,
    q_recv,
    c_send,
    c_recv,
    r_send,
    r_recv,
    g_send,
    g_recv,
):
    d = lax.axis_index("dp")
    f = lax.axis_index("fsdp")
    core = lax.rem(d, 2)
    xh = lax.rem(lax.div(d, 2), 2)
    z = lax.div(d, 4)
    par = lax.rem(f, 2)
    y = lax.div(f, 2)
    x = 2 * xh + par

    def dev(zz, xx, yy, cc):
        return (zz * 4 + lax.div(xx, 2) * 2 + cc, yy * 2 + lax.rem(xx, 2))

    def on_y(j):
        return dev(z, x, lax.rem(y + j, NY), core)

    def on_x(j):
        return dev(z, lax.rem(x + j, NX), y, core)

    def on_z(j):
        return dev(lax.rem(z + j, NZ), x, y, core)

    other = 1 - core
    mate = (d + 1 - 2 * core, f)

    def remote(src, dst, send, recv, target):
        return pltpu.make_async_remote_copy(
            src_ref=src,
            dst_ref=dst,
            send_sem=send,
            recv_sem=recv,
            device_id=target,
            device_id_type=MESH,
        )

    own_off = SHARD * f

    def shard_off(j):
        return SHARD * (2 * lax.rem(y + j, NY) + par)

    def rows(off, n):
        return pl.ds(pl.multiple_of(off, 32), n)

    def column(u):
        h = u // 7
        r = u % 7
        if r == 0:
            return MODEL + HEAD * (2 * core + h)
        if r == 1:
            return MODEL + 4 * HEAD + HEAD * (2 * core + h)
        return HEAD * (10 * core + 5 * h + r - 2)

    def lanes(off, n):
        return pl.ds(pl.multiple_of(off, HEAD), n)

    w_copies = []
    for u in range(UNITS):
        copy = pltpu.make_async_copy(
            w_hbm.at[:, lanes(column(u), HEAD)], wbuf.at[u, rows(own_off, SHARD), :], wsem.at[u]
        )
        copy.start()
        w_copies.append(copy)
        if u == 0:
            hid_copy = pltpu.make_async_copy(hid_hbm, hbuf, lsem.at[0])
            hid_copy.start()
    my_rows = rows(256 * core, 256)
    tgt_copy = pltpu.make_async_copy(
        tgt_hbm.at[:, lanes(1280 * core, 1280)], tbuf.at[my_rows, :], lsem.at[1]
    )
    tgt_copy.start()
    down_copy = pltpu.make_async_copy(down_hbm, down, lsem.at[2])
    down_copy.start()
    up_copy = pltpu.make_async_copy(up_hbm, up, lsem.at[3])
    up_copy.start()

    barrier = pltpu.get_barrier_semaphore()

    def greet(j, carry):
        pl.semaphore_signal(
            barrier, inc=1, device_id=(lax.rem(d + j, 32), f), device_id_type=MESH
        )
        return carry

    for j in (1, 2, 3):
        pl.semaphore_signal(barrier, inc=1, device_id=on_y(j), device_id_type=MESH)
    for j in (1, 3):
        pl.semaphore_signal(barrier, inc=1, device_id=on_x(j), device_id_type=MESH)
    lax.fori_loop(1, 32, greet, 0)

    lane = lax.broadcasted_iota(jnp.int32, (8, HEAD), 1)
    row = lax.broadcasted_iota(jnp.int32, (8, HEAD), 0)
    meta_own = jnp.where(
        row == 0,
        len_ref[0, 0].astype(F32),
        jnp.where(
            row == 1,
            len_ref[0, 1].astype(F32),
            jnp.where((row == 2) & (lane == grp_ref[0, 0]), F32(1.0), F32(0.0)),
        ),
    )
    meta[pl.ds(core, 1)] = meta_own[None]

    pl.semaphore_wait(barrier, 36)

    def piece(u, off, n):
        return wbuf.at[u, rows(off, n), :]

    def send_y(u, kind, off, n, target):
        ref = piece(u, off, n)
        remote(ref, ref, y_send.at[kind], y_recv.at[kind, u], target).start()

    def send_x(u, off):
        ref = piece(u, off, HALF)
        remote(ref, ref, x_send.at[0], x_recv.at[u], on_x(1)).start()

    def send_x_back(u, off):
        ref = piece(u, off + HALF, HALF)
        remote(ref, ref, x_send.at[1], x_recv.at[u], on_x(3)).start()

    def wait_y(u, kind, n):
        ref = wbuf.at[u, pl.ds(0, n), :]
        remote(ref, ref, y_send.at[kind], y_recv.at[kind, u], on_y(1)).wait_recv()

    def stage0(u):
        ref = wbuf.at[u, rows(own_off, SHARD), :]
        pltpu.make_async_copy(ref, ref, wsem.at[u]).wait()
        send_y(u, 0, own_off, SHARD, on_y(1))
        send_y(u, 1, own_off, SHARD, on_y(3))
        send_x(u, own_off)
        send_x_back(u, own_off)

    def stage1(u):
        wait_y(u, 0, SHARD)
        off = shard_off(3)
        send_y(u, 2, off, HALF, on_y(1))
        send_x(u, off)
        send_x_back(u, off)
        wait_y(u, 1, SHARD)
        off = shard_off(1)
        send_y(u, 3, off + HALF, HALF, on_y(3))
        send_x(u, off)
        send_x_back(u, off)

    def stage2(u):
        off = shard_off(2)
        wait_y(u, 2, HALF)
        send_x(u, off)
        wait_y(u, 3, HALF)
        send_x_back(u, off)

    def stage3(u):
        ref = wbuf.at[u, pl.ds(0, 8 * HALF), :]
        remote(ref, ref, x_send.at[0], x_recv.at[u], on_x(1)).wait_recv()

    def advance(u):
        @pl.when(u + AHEAD0 < UNITS)
        def _():
            stage0(u + AHEAD0)

        @pl.when(u + AHEAD1 < UNITS)
        def _():
            stage1(u + AHEAD1)

        @pl.when(u + AHEAD2 < UNITS)
        def _():
            stage2(u + AHEAD2)

        stage3(u)

    for u in range(AHEAD0):
        stage0(u)

    meta_copy = remote(
        meta.at[core], meta.at[core], d_send.at[0], d_recv.at[0], mate
    )
    meta_copy.start()
    tgt_remote = remote(
        tgt_hbm.at[:, lanes(1280 * other, 1280)],
        tbuf.at[my_rows, :],
        d_send.at[1],
        d_recv.at[1],
        mate,
    )
    tgt_remote.start()

    hid_copy.wait()
    gain = gain_ref[...]

    def norm_block(i, carry):
        values = hbuf[pl.ds(pl.multiple_of(32 * i, 32), 32), :].astype(F32)
        power = jnp.mean(values * values, -1, keepdims=True)
        out = (values * lax.rsqrt(power + EPS) * gain).astype(BF16)
        normed[rows(256 * core + 32 * i, 32), :] = out
        return carry

    lax.fori_loop(0, 8, norm_block, 0)
    normed_copy = remote(
        normed.at[my_rows, :], normed.at[my_rows, :], d_send.at[2], d_recv.at[2], mate
    )
    normed_copy.start()

    meta_copy.wait()
    cnt[0] = meta[0] + meta[1]

    def spread(step, count, place, buf):
        copies = []
        base = (0, 3, 6)[step]
        for j in range(1, count):
            copy = remote(
                cnt.at[step], buf.at[j - 1], c_send.at[base + j - 1], c_recv.at[base + j - 1], place(j)
            )
            copy.start()
            copies.append(copy)
        return copies

    def gathered(step, copies, buf):
        for copy in copies:
            copy.wait()
        cnt[step + 1] = cnt[step] + jnp.sum(buf[...], axis=0)

    copies_y = spread(0, NY, on_y, cbuf_y)
    stage1(0)

    down_copy.wait()
    up_copy.wait()
    key_at = lax.broadcasted_iota(jnp.int32, (HEAD, HEAD), 1)
    query_at = lax.broadcasted_iota(jnp.int32, (HEAD, HEAD), 0)
    for n in range(4):
        length = meta[n // 2, pl.ds(n % 2, 1), :]
        allowed = (key_at <= query_at) & (key_at.astype(F32) < length)
        mask[n] = jnp.where(allowed, F32(1.0), F32(0.0))
    tgt_copy.wait()
    tgt_remote.wait()
    for n in range(4):
        length = meta[n // 2, pl.ds(n % 2, 1), :]
        keep = query_at.astype(F32) < length
        for i in range(10):
            at = (pl.ds(HEAD * n, HEAD), pl.ds(HEAD * i, HEAD))
            tbuf[at] = jnp.where(keep, tbuf[at].astype(F32), F32(0.0)).astype(BF16)

    gathered(0, copies_y, cbuf_y)
    copies_x = spread(1, NX, on_x, cbuf_x)
    stage1(1)

    normed_copy.wait()
    low = mm(normed[...], down[...])
    lowq[...] = low[:, :RANK].astype(BF16)
    lowv[...] = low[:, RANK:].astype(BF16)
    for n in range(4):
        low_t[:, HEAD * n : HEAD * (n + 1)] = (
            low[HEAD * n : HEAD * (n + 1), :].astype(BF16).astype(F32).T
        )
    gathered(1, copies_x, cbuf_x)
    copies_z = spread(2, NZ, on_z, cbuf_z)
    stage2(0)

    sacc[...] = jnp.zeros_like(sacc)
    xsum[...] = jnp.zeros_like(xsum)

    def head_step(u, h, i):
        advance(u)
        qi = 5 * h + i
        base = mm(normed[...], wbuf[u])
        upq = up[rows(HEAD * (10 * core + qi), HEAD), :]
        upper = mm_nt(lowq[...], upq)
        qpol = (base + ADAPT_SCALE * upper).astype(BF16)
        qref = base.astype(BF16)
        grads = []
        for n in range(4):
            at = slice(HEAD * n, HEAD * (n + 1))
            keys = kbuf[h, at, :]
            values = vpol[h, at, :]
            both = jnp.concatenate([qpol[at], qref[at]], 0)
            scores = mm_nt(both, keys) * HEAD ** (-0.5)
            allowed = jnp.concatenate([mask[n], mask[n]], 0) > 0.0
            expo = jnp.where(allowed, jnp.exp(scores), F32(0.0))
            probs = expo * (1.0 / jnp.sum(expo, -1, keepdims=True))
            probs16 = probs.astype(BF16)
            pol = probs16[:HEAD]
            att_pol = mm(pol, values).astype(BF16).astype(F32)
            att_ref = mm(probs16[HEAD:], vref[h, at, :]).astype(BF16).astype(F32)
            target = tbuf[at, lanes(HEAD * qi, HEAD)]
            part = (att_pol - att_ref) * target.astype(F32)
            sacc[n] += jnp.sum(part.reshape(16, 8, HEAD), axis=0)
            d_probs = mm_nt(target, values)
            weighed = probs[:HEAD] * d_probs
            d_scores = weighed - probs[:HEAD] * jnp.sum(weighed, -1, keepdims=True)
            d_query = mm(d_scores.astype(BF16), keys).astype(BF16)
            grads.append(d_query)
            dvacc[at, :] += mm(probs[:HEAD].T.astype(BF16), target)
        d_query = jnp.concatenate(grads, 0)
        block = 10 * core + qi
        dq_all[block] = d_query
        remote(dq_all.at[block], dq_all.at[block], q_send.at[qi], q_recv.at[qi], mate).start()
        xsum[0:512, 0:RANK] += mm(d_query, upq)
        for j in range(2):
            at = lanes(HEAD * (2 * qi + j), HEAD)
            normed_t[at, :] = normed[:, at].T

    def group_step(h, carry):
        u = 7 * h
        advance(u)
        kbuf[h] = mm(normed[...], wbuf[u]).astype(BF16)
        advance(u + 1)
        base = mm(normed[...], wbuf[u + 1])
        upv = up[rows(MODEL + HEAD * (2 * core + h), HEAD), :]
        vref[h] = base.astype(BF16)
        vpol[h] = (base + ADAPT_SCALE * mm_nt(lowv[...], upv)).astype(BF16)
        dvacc[...] = jnp.zeros_like(dvacc)

        def inner(i, inner_carry):
            head_step(u + 2 + i, h, i)
            return inner_carry

        lax.fori_loop(0, 5, inner, 0)
        d_values = dvacc[...].astype(BF16)
        block = 20 + 2 * core + h
        dq_all[block] = d_values
        remote(
            dq_all.at[block], dq_all.at[block], q_send.at[10 + h], q_recv.at[10 + h], mate
        ).start()
        xsum[0:512, RANK:] += mm(d_values, upv)
        return carry

    lax.fori_loop(0, 2, group_step, 0)

    for n in range(4):
        xsum[512 + n : 513 + n, :] = jnp.sum(sacc[n], axis=0, keepdims=True)
    x_copy = remote(xsum, xrecv, d_send.at[3], d_recv.at[3], mate)
    x_copy.start()
    gathered(2, copies_z, cbuf_z)
    weights = []
    for c in range(2):
        count = jnp.sum(cnt[3, 2:3, :] * meta[c, 2:3, :], axis=-1, keepdims=True)
        weights.append(1.0 / (GROUPS * count))
    x_copy.wait()

    diffs = [
        jnp.sum(xsum[512 + n : 513 + n, :] + xrecv[512 + n : 513 + n, :], axis=-1, keepdims=True)
        * MODEL ** (-0.5)
        for n in range(4)
    ]
    coefs = []
    for c in range(2):
        margin = BETA * (diffs[2 * c] - diffs[2 * c + 1])
        loss = jnp.maximum(-margin, 0.0) + jnp.log1p(jnp.exp(-jnp.abs(margin)))
        slope = -(1.0 / (1.0 + jnp.exp(margin))) * weights[c] * BETA
        slope = slope * (ADAPT_SCALE * MODEL ** (-0.5))
        coefs += [slope, -slope]
        loss_ref[...] = loss if c == 0 else jnp.where(core == 1, loss, loss_ref[...])

    half_lane = lax.broadcasted_iota(jnp.int32, (1, HEAD), 1)
    half_row = lax.broadcasted_iota(jnp.int32, (HEAD, 1), 0)
    lane_scale = jnp.where(half_lane < RANK, F32(HEAD ** (-0.5)), F32(1.0))
    row_scale = jnp.where(half_row < RANK, F32(HEAD ** (-0.5)), F32(1.0))
    low_parts = []
    left_parts = []
    for n in range(4):
        at = slice(HEAD * n, HEAD * (n + 1))
        low_parts.append(((xsum[at, :] + xrecv[at, :]) * (lane_scale * coefs[n])).astype(BF16))
        low_t[:, at] = low_t[:, at] * (row_scale * coefs[n])
    d_low = jnp.concatenate(low_parts, 0)

    def share_a(j, carry):
        left = normed_t[rows(SHARD * j + HALF * core, HALF), :]
        red[j, 0:HALF, :] = mm(left, d_low).astype(BF16)
        return carry

    lax.fori_loop(0, 8, share_a, 0)

    def mate_blocks(i, carry):
        @pl.when(i < 10)
        def _():
            block = 10 * other + i
            remote(
                dq_all.at[10 * core + i], dq_all.at[block], q_send.at[i], q_recv.at[i], mate
            ).wait()

        @pl.when(i >= 10)
        def _():
            block = 20 + 2 * other + i - 10
            remote(
                dq_all.at[20 + 2 * core + i - 10], dq_all.at[block], q_send.at[i], q_recv.at[i], mate
            ).wait()

        return carry

    lax.fori_loop(0, 12, mate_blocks, 0)
    left_q = low_t[rows(32 * core, 32), :].astype(BF16)
    left_v = low_t[rows(RANK + 32 * core, 32), :].astype(BF16)
    for b in range(24):
        left = left_q if b < 20 else left_v
        at = HALF + 32 * (b % 3)
        red[b // 3, at : at + 32, :] = mm(left, dq_all[b]).astype(BF16)

    def exchange(step, count, place, source, buf):
        copies = []
        base = (0, 3, 6)[step]
        for j in range(1, count):
            copy = remote(
                source(j), buf.at[j - 1], r_send.at[base + j - 1], r_recv.at[base + j - 1], place(j)
            )
            copy.start()
            copies.append(copy)
        for copy in copies:
            copy.wait()

    exchange(0, NY, on_y, lambda j: red.at[pl.ds(2 * lax.rem(y + j, NY), 2)], ry)
    total = red[pl.ds(2 * y, 2)].astype(F32)
    for j in range(NY - 1):
        total += ry[j].astype(F32)
    red1[...] = total.astype(BF16)

    def x_part(j):
        xx = lax.rem(x + j, NX)
        return red1.at[lax.rem(xx, 2), rows(HEAD * lax.div(xx, 2), HEAD), :]

    exchange(1, NX, on_x, x_part, rx)
    total = red1[par, rows(HEAD * xh, HEAD), :].astype(F32)
    for j in range(NX - 1):
        total += rx[j].astype(F32)
    red2[...] = total.astype(BF16)

    def z_part(j):
        return red2.at[pl.ds(pl.multiple_of(16 * lax.rem(z + j, NZ), 16), 16), :]

    exchange(2, NZ, on_z, z_part, rz)
    total = red2[pl.ds(pl.multiple_of(16 * z, 16), 16), :].astype(F32)
    for j in range(NZ - 1):
        total += rz[j].astype(F32)
    mine = pl.ds(pl.multiple_of(HEAD * xh + 16 * z, 16), 16)
    fin[core, mine, :] = total.astype(BF16)

    def hand_out(j, carry):
        ref = fin.at[core, mine, :]
        remote(ref, ref, g_send.at[0], g_recv.at[0], (lax.rem(d + j, 32), f)).start()
        return carry

    lax.fori_loop(1, 32, hand_out, 0)
    whole = wbuf.at[0, pl.ds(0, 31 * 16), :]
    remote(whole, whole, g_send.at[0], g_recv.at[0], mate).wait()

    parts = [[], [], []]
    for c in range(2):
        ga_ref[HALF * c : HALF * (c + 1), :] = fin[c, 0:HALF, :].astype(F32)
        for i in range(3):
            at = HALF + 32 * i
            parts[i].append(fin[c, at : at + 32, :].astype(F32))
    for i in range(3):
        gb_ref[HEAD * i : HEAD * (i + 1), :] = jnp.concatenate(parts[i], 0).T

    whole = wbuf.at[:, pl.ds(0, SHARD), :]
    for kind in (0, 1):
        remote(whole, whole, y_send.at[kind], y_recv.at[kind, 0], mate).wait_send()
    whole = wbuf.at[:, pl.ds(0, HALF), :]
    for kind in (2, 3):
        remote(whole, whole, y_send.at[kind], y_recv.at[kind, 0], mate).wait_send()
    whole = wbuf.at[:, pl.ds(0, 4 * HALF), :]
    for kind in (0, 1):
        remote(whole, whole, x_send.at[kind], x_recv.at[0], mate).wait_send()


def fused(lengths, groups, gain, hidden, targets, weight, adapter_down, adapter_up):
    any_spec = pl.BlockSpec(memory_space=pl.ANY)
    smem = pl.BlockSpec(memory_space=pltpu.SMEM)
    vmem = pl.BlockSpec(memory_space=pltpu.VMEM)
    dma = pltpu.SemaphoreType.DMA
    return pl.pallas_call(
        kernel,
        out_shape=(
            jax.ShapeDtypeStruct((1, 1), F32),
            jax.ShapeDtypeStruct((SHARD, HEAD), F32),
            jax.ShapeDtypeStruct((3 * HEAD, RANK), F32),
        ),
        in_specs=[smem, smem, vmem, any_spec, any_spec, any_spec, any_spec, any_spec],
        out_specs=(vmem, vmem, vmem),
        scratch_shapes=[
            pltpu.VMEM((UNITS, MODEL, HEAD), BF16),
            pltpu.VMEM((256, MODEL), BF16),
            pltpu.VMEM((512, MODEL), BF16),
            pltpu.VMEM((MODEL, 512), BF16),
            pltpu.VMEM((512, 1280), BF16),
            pltpu.VMEM((MODEL, HEAD), BF16),
            pltpu.VMEM((3072, RANK), BF16),
            pltpu.VMEM((512, RANK), BF16),
            pltpu.VMEM((512, RANK), BF16),
            pltpu.VMEM((HEAD, 512), F32),
            pltpu.VMEM((2, 512, HEAD), BF16),
            pltpu.VMEM((2, 512, HEAD), BF16),
            pltpu.VMEM((2, 512, HEAD), BF16),
            pltpu.VMEM((4, HEAD, HEAD), F32),
            pltpu.VMEM((4, 8, HEAD), F32),
            pltpu.VMEM((512, HEAD), F32),
            pltpu.VMEM((24, 512, HEAD), BF16),
            pltpu.VMEM((520, HEAD), F32),
            pltpu.VMEM((520, HEAD), F32),
            pltpu.VMEM((2, 8, HEAD), F32),
            pltpu.VMEM((4, 8, HEAD), F32),
            pltpu.VMEM((NY - 1, 8, HEAD), F32),
            pltpu.VMEM((NX - 1, 8, HEAD), F32),
            pltpu.VMEM((NZ - 1, 8, HEAD), F32),
            pltpu.VMEM((8, 256, HEAD), BF16),
            pltpu.VMEM((2, 256, HEAD), BF16),
            pltpu.VMEM((HEAD, HEAD), BF16),
            pltpu.VMEM((NY - 1, 2, 256, HEAD), BF16),
            pltpu.VMEM((NX - 1, HEAD, HEAD), BF16),
            pltpu.VMEM((NZ - 1, 16, HEAD), BF16),
            pltpu.VMEM((2, 256, HEAD), BF16),
            dma((UNITS,)),
            dma((4,)),
            dma((4,)),
            dma((4, UNITS)),
            dma((2,)),
            dma((UNITS,)),
            dma((4,)),
            dma((4,)),
            dma((12,)),
            dma((12,)),
            dma((13,)),
            dma((13,)),
            dma((13,)),
            dma((13,)),
            dma((1,)),
            dma((1,)),
        ],
        compiler_params=pltpu.CompilerParams(
            collective_id=0, has_side_effects=True, vmem_limit_bytes=56 * 1024 * 1024
        ),
        cost_estimate=pl.CostEstimate(
            flops=8_000_000_000, bytes_accessed=8_000_000, transcendentals=1_400_000
        ),
    )(lengths, groups, gain, hidden, targets, weight, adapter_down, adapter_up)


def body(
    hidden,
    targets,
    lengths,
    prompt_group_index,
    input_norm_gain,
    frozen_weight,
    adapter_down,
    adapter_up,
):
    losses, grad_a, grad_b = fused(
        lengths,
        prompt_group_index,
        input_norm_gain.reshape(1, MODEL),
        hidden.reshape(256, MODEL),
        targets.reshape(256, MODEL),
        frozen_weight,
        adapter_down,
        adapter_up,
    )
    return (losses.reshape(1), grad_a, grad_b)


def solution(mesh):
    return jax.shard_map(
        body,
        mesh=mesh,
        in_specs=(
            P(("dp", "fsdp"), None, None, None),
            P(("dp", "fsdp"), None, None, None),
            P(("dp", "fsdp"), None),
            P(("dp", "fsdp"), None),
            P(),
            P("fsdp", None),
            P(),
            P(),
        ),
        out_specs=(P(("dp", "fsdp")), P("fsdp", None), P("fsdp", None)),
        check_vma=False,
    )
```

```python
import jax
import jax.numpy as jnp
from jax import lax
from jax.experimental import pallas as pl
from jax.experimental.pallas import tpu as pltpu
from jax.sharding import PartitionSpec as P

MODEL = 2560
HEAD = 128
RANK = 64
GROUPS = 16
EPS = 1e-05
BETA = 0.1
ADAPT_SCALE = 0.5

NZ, NX, NY = 8, 4, 4
SHARD = 320
HALF = 160
UNITS = 14
SPLIT_UNITS = 12
SPLITS = 4
AHEAD0, AHEAD1, AHEAD2, AHEADZ = 9, 7, 5, 3
BURST = 2

MESH = pl.DeviceIdType.MESH
F32 = jnp.float32
BF16 = jnp.bfloat16


def mm(a, b):
    return lax.dot_general(a, b, (((1,), (0,)), ((), ())), preferred_element_type=F32)


def mm_nt(a, b):
    return lax.dot_general(a, b, (((1,), (1,)), ((), ())), preferred_element_type=F32)


def kernel(
    len_ref,
    grp_ref,
    gain_ref,
    hid_hbm,
    tgt_hbm,
    w_hbm,
    down_hbm,
    up_t_hbm,
    loss_ref,
    fin_ref,
    wbuf,
    hbuf,
    normed,
    normed_t,
    tbuf,
    down,
    up_t,
    lowq,
    lowv,
    low_t,
    left,
    kbuf,
    k_t,
    vcat,
    mask,
    dvacc,
    dq_all,
    xsum,
    xrecv,
    meta,
    cnt,
    cbuf_y,
    cbuf_x,
    cbuf_z,
    red,
    red1,
    red2,
    ry,
    rx,
    rz,
    fin,
    wsem,
    lsem,
    y_send,
    y_recv,
    x_send,
    x_recv,
    z_send,
    z_recv,
    d_send,
    d_recv,
    q_send,
    q_recv,
    c_send,
    c_recv,
    r_send,
    r_recv,
    g_send,
    g_recv,
):
    d = lax.axis_index("dp")
    f = lax.axis_index("fsdp")
    core = lax.rem(d, 2)
    xh = lax.rem(lax.div(d, 2), 2)
    z = lax.div(d, 4)
    par = lax.rem(f, 2)
    y = lax.div(f, 2)
    x = 2 * xh + par

    def dev(zz, xx, yy, cc):
        return (zz * 4 + lax.div(xx, 2) * 2 + cc, yy * 2 + lax.rem(xx, 2))

    def on_y(j):
        return dev(z, x, lax.rem(y + j, NY), core)

    def on_x(j):
        return dev(z, lax.rem(x + j, NX), y, core)

    def on_z(j):
        return dev(lax.rem(z + j, NZ), x, y, core)

    other = 1 - core
    mate = (d + 1 - 2 * core, f)

    def remote(src, dst, send, recv, target):
        return pltpu.make_async_remote_copy(
            src_ref=src,
            dst_ref=dst,
            send_sem=send,
            recv_sem=recv,
            device_id=target,
            device_id_type=MESH,
        )

    own_off = SHARD * f

    def shard_off(j):
        return SHARD * (2 * lax.rem(y + j, NY) + par)

    def rows(off, n):
        return pl.ds(pl.multiple_of(off, 32), n)

    def column(u):
        h = u // 7
        r = u % 7
        if r == 0:
            return MODEL + HEAD * (2 * core + h)
        if r == 1:
            return MODEL + 4 * HEAD + HEAD * (2 * core + h)
        return HEAD * (10 * core + 5 * h + r - 2)

    def lanes(off, n):
        return pl.ds(pl.multiple_of(off, HEAD), n)

    w_copies = []
    for u in range(UNITS):
        copy = pltpu.make_async_copy(
            w_hbm.at[:, lanes(column(u), HEAD)], wbuf.at[u, rows(own_off, SHARD), :], wsem.at[u]
        )
        copy.start()
        w_copies.append(copy)
        if u == 0:
            hid_copy = pltpu.make_async_copy(hid_hbm, hbuf, lsem.at[0])
            hid_copy.start()
    my_rows = rows(256 * core, 256)
    tgt_copy = pltpu.make_async_copy(
        tgt_hbm.at[:, lanes(1280 * core, 1280)], tbuf.at[my_rows, :], lsem.at[1]
    )
    tgt_copy.start()
    down_copy = pltpu.make_async_copy(down_hbm, down, lsem.at[2])
    down_copy.start()
    up_copy = pltpu.make_async_copy(up_t_hbm, up_t, lsem.at[3])
    up_copy.start()

    barrier = pltpu.get_barrier_semaphore()

    def greet(j, carry):
        pl.semaphore_signal(
            barrier, inc=1, device_id=(lax.rem(d + j, 32), f), device_id_type=MESH
        )
        return carry

    for j in (1, 2, 3):
        pl.semaphore_signal(barrier, inc=1, device_id=on_y(j), device_id_type=MESH)
    for j in (1, 3):
        pl.semaphore_signal(barrier, inc=1, device_id=on_x(j), device_id_type=MESH)
    lax.fori_loop(1, 32, greet, 0)

    lane = lax.broadcasted_iota(jnp.int32, (8, HEAD), 1)
    row = lax.broadcasted_iota(jnp.int32, (8, HEAD), 0)
    meta_own = jnp.where(
        row == 0,
        len_ref[0, 0].astype(F32),
        jnp.where(
            row == 1,
            len_ref[0, 1].astype(F32),
            jnp.where((row == 2) & (lane == grp_ref[0, 0]), F32(1.0), F32(0.0)),
        ),
    )
    meta[pl.ds(core, 1)] = meta_own[None]

    pl.semaphore_wait(barrier, 36)

    def piece(u, off, n):
        return wbuf.at[u, rows(off, n), :]

    def send_y(u, kind, off, n, target):
        ref = piece(u, off, n)
        remote(ref, ref, y_send.at[kind], y_recv.at[kind, u], target).start()

    def send_x(u, off):
        ref = piece(u, off, HALF)
        remote(ref, ref, x_send.at[0], x_recv.at[u], on_x(1)).start()

    def send_x_back(u, off):
        ref = piece(u, off + HALF, HALF)
        remote(ref, ref, x_send.at[1], x_recv.at[u], on_x(3)).start()

    def wait_y(u, kind, n):
        ref = wbuf.at[u, pl.ds(0, n), :]
        remote(ref, ref, y_send.at[kind], y_recv.at[kind, u], on_y(1)).wait_recv()

    z_par = lax.rem(z, 2)

    def split(u):
        return (u < SPLIT_UNITS) & (lax.rem(u, 3) < 2)

    def takes(u):
        return split(u) & (lax.rem(u, 3) != z_par)

    def gives(u):
        return split(u) & (lax.rem(u, 3) == z_par)

    def wait_own(u):
        ref = wbuf.at[u, rows(own_off, SHARD), :]
        pltpu.make_async_copy(ref, ref, wsem.at[u]).wait()

    def stage0(u):
        @pl.when(jnp.logical_not(takes(u)))
        def _():
            wait_own(u)
            send_y(u, 0, own_off, SHARD, on_y(1))
            send_y(u, 1, own_off, SHARD, on_y(3))
            send_x(u, own_off)
            send_x_back(u, own_off)

    def stage1(u):
        @pl.when(jnp.logical_not(takes(u)))
        def _():
            wait_y(u, 0, SHARD)
            off = shard_off(3)
            send_y(u, 2, off, HALF, on_y(1))
            send_x(u, off)
            send_x_back(u, off)
            wait_y(u, 1, SHARD)
            off = shard_off(1)
            send_y(u, 3, off + HALF, HALF, on_y(3))
            send_x(u, off)
            send_x_back(u, off)

    def stage2(u):
        @pl.when(jnp.logical_not(takes(u)))
        def _():
            off = shard_off(2)
            wait_y(u, 2, HALF)
            send_x(u, off)
            wait_y(u, 3, HALF)
            send_x_back(u, off)

    def wait_x(u):
        ref = wbuf.at[u, pl.ds(0, 8 * HALF), :]
        remote(ref, ref, x_send.at[0], x_recv.at[u], on_x(1)).wait_recv()

    def send_z(u, way, off, n):
        ref = piece(u, off, n)
        remote(ref, ref, z_send.at[way], z_recv.at[u], on_z((1, NZ - 1)[way])).start()

    def stage_z(u):
        @pl.when(gives(u))
        def _():
            wait_x(u)
            for j in range(1, 8):
                off = SHARD * lax.rem(f + j, 8)
                if j == 4:
                    send_z(u, 0, off, HALF)
                    send_z(u, 1, off + HALF, HALF)
                else:
                    send_z(u, 0 if j < 4 else 1, off, SHARD)

    def stage3(u):
        @pl.when(takes(u))
        def _():
            wait_own(u)
            ref = wbuf.at[u, pl.ds(0, 7 * SHARD), :]
            remote(ref, ref, z_send.at[0], z_recv.at[u], on_z(1)).wait_recv()

        @pl.when(jnp.logical_not(split(u)))
        def _():
            wait_x(u)

    def advance(u):
        for stage, ahead in (
            (stage0, AHEAD0),
            (stage1, AHEAD1),
            (stage2, AHEAD2),
            (stage_z, AHEADZ),
        ):

            @pl.when(u + ahead < UNITS)
            def _(stage=stage, ahead=ahead):
                stage(u + ahead)

        stage3(u)

    def early(tick):
        for stage, ahead in (
            (stage0, AHEAD0),
            (stage1, AHEAD1),
            (stage2, AHEAD2),
            (stage_z, AHEADZ),
        ):
            if 0 <= tick + ahead < UNITS:
                stage(tick + ahead)

    ticks = iter(range(-AHEAD0, 0))
    for _ in range(BURST):
        early(next(ticks))

    meta_copy = remote(meta.at[core], meta.at[core], d_send.at[0], d_recv.at[0], mate)
    meta_copy.start()
    tgt_remote = remote(
        tgt_hbm.at[:, lanes(1280 * other, 1280)],
        tbuf.at[my_rows, :],
        d_send.at[1],
        d_recv.at[1],
        mate,
    )
    tgt_remote.start()

    hid_copy.wait()
    gain = gain_ref[...].reshape(1, MODEL)

    def norm_block(i, carry):
        values = hbuf[pl.ds(pl.multiple_of(32 * i, 32), 32), :].astype(F32)
        power = jnp.mean(values * values, -1, keepdims=True)
        out = (values * lax.rsqrt(power + EPS) * gain).astype(BF16)
        normed[rows(256 * core + 32 * i, 32), :] = out
        return carry

    lax.fori_loop(0, 8, norm_block, 0)
    normed_copy = remote(
        normed.at[my_rows, :], normed.at[my_rows, :], d_send.at[2], d_recv.at[2], mate
    )
    normed_copy.start()
    early(next(ticks))

    meta_copy.wait()
    cnt[0] = meta[0] + meta[1]

    def spread(step, count, place, buf):
        copies = []
        base = (0, 3, 6)[step]
        for j in range(1, count):
            copy = remote(
                cnt.at[step], buf.at[j - 1], c_send.at[base + j - 1], c_recv.at[base + j - 1], place(j)
            )
            copy.start()
            copies.append(copy)
        return copies

    def gathered(step, copies, buf):
        for copy in copies:
            copy.wait()
        cnt[step + 1] = cnt[step] + jnp.sum(buf[...], axis=0)

    copies_y = spread(0, NY, on_y, cbuf_y)
    early(next(ticks))

    key_at = lax.broadcasted_iota(jnp.int32, (HEAD, HEAD), 0)
    query_at = lax.broadcasted_iota(jnp.int32, (HEAD, HEAD), 1)
    for n in range(4):
        length = meta[n // 2, pl.ds(n % 2, 1), :]
        allowed = (key_at <= query_at) & (key_at.astype(F32) < length)
        mask[n] = jnp.where(allowed, F32(1.0), F32(0.0))
    tgt_copy.wait()
    tgt_remote.wait()
    for n in range(4):
        length = meta[n // 2, pl.ds(n % 2, 1), :]
        keep = key_at.astype(F32) < length
        for i in range(10):
            at = (pl.ds(HEAD * n, HEAD), pl.ds(HEAD * i, HEAD))
            tbuf[at] = jnp.where(keep, tbuf[at].astype(F32), F32(0.0)).astype(BF16)
    early(next(ticks))

    gathered(0, copies_y, cbuf_y)
    copies_x = spread(1, NX, on_x, cbuf_x)

    down_copy.wait()
    up_copy.wait()
    normed_copy.wait()
    low = mm(normed[...], down[...])
    lowq[...] = low[:, :RANK].astype(BF16)
    lowv[...] = low[:, RANK:].astype(BF16)
    for n in range(4):
        low_t[:, HEAD * n : HEAD * (n + 1)] = (
            low[HEAD * n : HEAD * (n + 1), :].astype(BF16).astype(F32).T
        )
    xsum[...] = jnp.zeros_like(xsum)
    early(next(ticks))
    gathered(1, copies_x, cbuf_x)
    copies_z = spread(2, NZ, on_z, cbuf_z)
    for tick in ticks:
        early(tick)

    def head_step(u, h, i):
        advance(u)
        qi = 5 * h + i
        block = 10 * core + qi
        base = mm(normed[...], wbuf[u])
        upq = up_t[:, lanes(HEAD * block, HEAD)]
        qpol = (base + ADAPT_SCALE * mm(lowq[...], upq)).astype(BF16)
        qref = base.astype(BF16)
        for n in range(4):
            at = slice(HEAD * n, HEAD * (n + 1))
            both = jnp.concatenate([qpol[at], qref[at]], 0)
            scores = mm_nt(kbuf[h, at, :], both) * HEAD ** (-0.5)
            allowed = jnp.concatenate([mask[n], mask[n]], 1) > 0.0
            expo = jnp.where(allowed, jnp.exp(scores), F32(0.0))
            probs = expo * (1.0 / jnp.sum(expo, 0, keepdims=True))
            target = tbuf[at, lanes(HEAD * qi, HEAD)]
            d_both = mm_nt(vcat[h, n], target)
            pol = probs[:, :HEAD]
            weighed = pol * d_both[:HEAD]
            token = jnp.sum(weighed, 0, keepdims=True)
            token_ref = jnp.sum(probs[:, HEAD:] * d_both[HEAD:], 0, keepdims=True)
            xsum[HEAD : HEAD + 1, at] += token - token_ref
            d_scores = (weighed - pol * token).astype(BF16)
            dq_all[block, :, at] = mm(k_t[h, :, at], d_scores).astype(BF16)
            dvacc[at, :] += mm(pol.astype(BF16), target)
        remote(dq_all.at[block], dq_all.at[block], q_send.at[qi], q_recv.at[qi], mate).start()
        xsum[0:RANK, :] += mm(upq, dq_all[block])
        for j in range(2):
            at = lanes(HEAD * (2 * qi + j), HEAD)
            normed_t[at, :] = normed[:, at].T

    def group_step(h, carry):
        u = 7 * h
        advance(u)
        keys = mm(normed[...], wbuf[u]).astype(BF16)
        kbuf[h] = keys
        for n in range(4):
            at = slice(HEAD * n, HEAD * (n + 1))
            k_t[h, :, at] = keys[at].astype(F32).T.astype(BF16)
        advance(u + 1)
        base = mm(normed[...], wbuf[u + 1])
        block = 20 + 2 * core + h
        upv = up_t[:, lanes(HEAD * block, HEAD)]
        values = (base + ADAPT_SCALE * mm(lowv[...], upv)).astype(BF16)
        for n in range(4):
            at = slice(HEAD * n, HEAD * (n + 1))
            vcat[h, n, 0:HEAD] = values[at]
            vcat[h, n, HEAD:] = base[at].astype(BF16)
        dvacc[...] = jnp.zeros_like(dvacc)

        def inner(i, inner_carry):
            head_step(u + 2 + i, h, i)
            return inner_carry

        lax.fori_loop(0, 5, inner, 0)
        for n in range(4):
            at = slice(HEAD * n, HEAD * (n + 1))
            dq_all[block, :, at] = dvacc[at, :].T.astype(BF16)
        remote(
            dq_all.at[block], dq_all.at[block], q_send.at[10 + h], q_recv.at[10 + h], mate
        ).start()
        xsum[RANK:HEAD, :] += mm(upv, dq_all[block])
        return carry

    lax.fori_loop(0, 2, group_step, 0)

    x_copy = remote(xsum, xrecv, d_send.at[3], d_recv.at[3], mate)
    x_copy.start()
    gathered(2, copies_z, cbuf_z)
    weights = []
    for c in range(2):
        count = jnp.sum(cnt[3, 2:3, :] * meta[c, 2:3, :], axis=-1, keepdims=True)
        weights.append(1.0 / (GROUPS * count))
    x_copy.wait()

    differ = xsum[HEAD : HEAD + 1, :] + xrecv[HEAD : HEAD + 1, :]
    diffs = [
        jnp.sum(differ[:, HEAD * n : HEAD * (n + 1)], axis=-1, keepdims=True) * MODEL ** (-0.5)
        for n in range(4)
    ]
    coefs = []
    for c in range(2):
        margin = BETA * (diffs[2 * c] - diffs[2 * c + 1])
        loss = jnp.maximum(-margin, 0.0) + jnp.log1p(jnp.exp(-jnp.abs(margin)))
        slope = -(1.0 / (1.0 + jnp.exp(margin))) * weights[c] * BETA
        slope = slope * (ADAPT_SCALE * MODEL ** (-0.5))
        coefs += [slope, -slope]
        loss_ref[...] = loss if c == 0 else jnp.where(core == 1, loss, loss_ref[...])

    half_row = lax.broadcasted_iota(jnp.int32, (HEAD, 1), 0)
    row_scale = jnp.where(half_row < RANK, F32(HEAD ** (-0.5)), F32(1.0))
    low_parts = []
    for n in range(4):
        at = slice(HEAD * n, HEAD * (n + 1))
        scale = row_scale * coefs[n]
        low_parts.append(((xsum[0:HEAD, at] + xrecv[0:HEAD, at]) * scale).astype(BF16))
        low_t[:, at] = low_t[:, at] * scale
    d_low = jnp.concatenate(low_parts, 1)
    left[0] = low_t[rows(32 * core, 32), :].astype(BF16)
    left[1] = low_t[rows(RANK + 32 * core, 32), :].astype(BF16)

    def mate_blocks(i, carry):
        @pl.when(i < 10)
        def _():
            mine = dq_all.at[10 * core + i]
            remote(mine, mine, q_send.at[i], q_recv.at[i], mate).wait()

        @pl.when(i >= 10)
        def _():
            mine = dq_all.at[20 + 2 * core + i - 10]
            remote(mine, mine, q_send.at[i], q_recv.at[i], mate).wait()

        return carry

    lax.fori_loop(0, 12, mate_blocks, 0)

    copies = []
    for k in (2, 1, 3, 0):
        yy = lax.rem(y + k, NY)
        for q in range(2):
            j = 2 * yy + q
            part = normed_t[rows(SHARD * j + HALF * core, HALF), :]
            red[j, 0:HALF, :] = mm_nt(part, d_low).astype(BF16)
            for i in range(3):
                b = 3 * j + i
                which = (b >= 20).astype(jnp.int32)
                at = HALF + 32 * i
                red[j, at : at + 32, :] = mm_nt(left[which], dq_all[b]).astype(BF16)
        if k:
            copy = remote(
                red.at[pl.ds(2 * yy, 2)], ry.at[k - 1], r_send.at[k - 1], r_recv.at[k - 1], on_y(k)
            )
            copy.start()
            copies.append(copy)
    for copy in copies:
        copy.wait()

    def exchange(step, count, place, source, buf):
        copies = []
        base = (0, 3, 6)[step]
        for j in range(1, count):
            copy = remote(
                source(j), buf.at[j - 1], r_send.at[base + j - 1], r_recv.at[base + j - 1], place(j)
            )
            copy.start()
            copies.append(copy)
        for copy in copies:
            copy.wait()

    total = red[pl.ds(2 * y, 2)].astype(F32)
    for j in range(NY - 1):
        total += ry[j].astype(F32)
    red1[...] = total.astype(BF16)

    def x_part(j):
        xx = lax.rem(x + j, NX)
        return red1.at[lax.rem(xx, 2), rows(HEAD * lax.div(xx, 2), HEAD), :]

    exchange(1, NX, on_x, x_part, rx)
    total = red1[par, rows(HEAD * xh, HEAD), :].astype(F32)
    for j in range(NX - 1):
        total += rx[j].astype(F32)
    red2[...] = total.astype(BF16)

    def z_part(j):
        return red2.at[pl.ds(pl.multiple_of(16 * lax.rem(z + j, NZ), 16), 16), :]

    exchange(2, NZ, on_z, z_part, rz)
    total = red2[pl.ds(pl.multiple_of(16 * z, 16), 16), :].astype(F32)
    for j in range(NZ - 1):
        total += rz[j].astype(F32)
    mine = pl.ds(pl.multiple_of(HEAD * xh + 16 * z, 16), 16)
    fin[core, mine, :] = total.astype(BF16)

    def hand_out(j, carry):
        ref = fin.at[core, mine, :]
        remote(ref, ref, g_send.at[0], g_recv.at[0], (lax.rem(d + j, 32), f)).start()
        return carry

    lax.fori_loop(1, 32, hand_out, 0)
    whole = wbuf.at[0, pl.ds(0, 31 * 16), :]
    remote(whole, whole, g_send.at[0], g_recv.at[0], mate).wait()

    fin_ref[...] = fin[...]

    sent = UNITS - SPLITS
    whole = wbuf.at[pl.ds(0, sent), pl.ds(0, SHARD), :]
    for kind in (0, 1):
        remote(whole, whole, y_send.at[kind], y_recv.at[kind, 0], mate).wait_send()
    whole = wbuf.at[pl.ds(0, sent), pl.ds(0, HALF), :]
    for kind in (2, 3):
        remote(whole, whole, y_send.at[kind], y_recv.at[kind, 0], mate).wait_send()
    whole = wbuf.at[pl.ds(0, sent), pl.ds(0, 4 * HALF), :]
    for kind in (0, 1):
        remote(whole, whole, x_send.at[kind], x_recv.at[0], mate).wait_send()
    whole = wbuf.at[pl.ds(0, SPLITS), pl.ds(0, 7 * HALF), :]
    for way in (0, 1):
        remote(whole, whole, z_send.at[way], z_recv.at[0], mate).wait_send()


def fused(lengths, groups, gain, hidden, targets, weight, adapter_down, adapter_up_t):
    any_spec = pl.BlockSpec(memory_space=pl.ANY)
    smem = pl.BlockSpec(memory_space=pltpu.SMEM)
    vmem = pl.BlockSpec(memory_space=pltpu.VMEM)
    dma = pltpu.SemaphoreType.DMA
    return pl.pallas_call(
        kernel,
        out_shape=(
            jax.ShapeDtypeStruct((1, 1), F32),
            jax.ShapeDtypeStruct((2, 256, HEAD), BF16),
        ),
        in_specs=[smem, smem, vmem, any_spec, any_spec, any_spec, any_spec, any_spec],
        out_specs=(vmem, vmem),
        scratch_shapes=[
            pltpu.VMEM((UNITS, MODEL, HEAD), BF16),
            pltpu.VMEM((256, MODEL), BF16),
            pltpu.VMEM((512, MODEL), BF16),
            pltpu.VMEM((MODEL, 512), BF16),
            pltpu.VMEM((512, 1280), BF16),
            pltpu.VMEM((MODEL, HEAD), BF16),
            pltpu.VMEM((RANK, 3072), BF16),
            pltpu.VMEM((512, RANK), BF16),
            pltpu.VMEM((512, RANK), BF16),
            pltpu.VMEM((HEAD, 512), F32),
            pltpu.VMEM((2, 32, 512), BF16),
            pltpu.VMEM((2, 512, HEAD), BF16),
            pltpu.VMEM((2, HEAD, 512), BF16),
            pltpu.VMEM((2, 4, 256, HEAD), BF16),
            pltpu.VMEM((4, HEAD, HEAD), F32),
            pltpu.VMEM((512, HEAD), F32),
            pltpu.VMEM((24, HEAD, 512), BF16),
            pltpu.VMEM((136, 512), F32),
            pltpu.VMEM((136, 512), F32),
            pltpu.VMEM((2, 8, HEAD), F32),
            pltpu.VMEM((4, 8, HEAD), F32),
            pltpu.VMEM((NY - 1, 8, HEAD), F32),
            pltpu.VMEM((NX - 1, 8, HEAD), F32),
            pltpu.VMEM((NZ - 1, 8, HEAD), F32),
            pltpu.VMEM((8, 256, HEAD), BF16),
            pltpu.VMEM((2, 256, HEAD), BF16),
            pltpu.VMEM((HEAD, HEAD), BF16),
            pltpu.VMEM((NY - 1, 2, 256, HEAD), BF16),
            pltpu.VMEM((NX - 1, HEAD, HEAD), BF16),
            pltpu.VMEM((NZ - 1, 16, HEAD), BF16),
            pltpu.VMEM((2, 256, HEAD), BF16),
            dma((UNITS,)),
            dma((4,)),
            dma((4,)),
            dma((4, UNITS)),
            dma((2,)),
            dma((UNITS,)),
            dma((2,)),
            dma((UNITS,)),
            dma((4,)),
            dma((4,)),
            dma((12,)),
            dma((12,)),
            dma((13,)),
            dma((13,)),
            dma((13,)),
            dma((13,)),
            dma((1,)),
            dma((1,)),
        ],
        compiler_params=pltpu.CompilerParams(
            collective_id=0, has_side_effects=True, vmem_limit_bytes=56 * 1024 * 1024
        ),
        cost_estimate=pl.CostEstimate(
            flops=8_000_000_000, bytes_accessed=8_000_000, transcendentals=1_400_000
        ),
    )(lengths, groups, gain, hidden, targets, weight, adapter_down, adapter_up_t)


def finish_kernel(fin_ref, ga_ref, gb_t_ref):
    for c in range(2):
        ga_ref[HALF * c : HALF * (c + 1), :] = fin_ref[c, 0:HALF, :].astype(F32)
        for i in range(3):
            at = HALF + 32 * i
            gb_t_ref[32 * c : 32 * (c + 1), HEAD * i : HEAD * (i + 1)] = fin_ref[
                c, at : at + 32, :
            ].astype(F32)


def finish(fin):
    vmem = pl.BlockSpec(memory_space=pltpu.VMEM)
    return pl.pallas_call(
        finish_kernel,
        out_shape=(
            jax.ShapeDtypeStruct((SHARD, HEAD), F32),
            jax.ShapeDtypeStruct((RANK, 3 * HEAD), F32),
        ),
        in_specs=[vmem],
        out_specs=(vmem, vmem),
    )(fin)


def body(
    hidden,
    targets,
    lengths,
    prompt_group_index,
    input_norm_gain,
    frozen_weight,
    adapter_down,
    adapter_up,
):
    losses, fin = fused(
        lengths,
        prompt_group_index,
        input_norm_gain,
        hidden.reshape(256, MODEL),
        targets.reshape(256, MODEL),
        frozen_weight,
        adapter_down,
        adapter_up.T,
    )
    grad_a, grad_b_t = finish(fin)
    return (losses.reshape(1), grad_a, grad_b_t.T)


def solution(mesh):
    return jax.shard_map(
        body,
        mesh=mesh,
        in_specs=(
            P(("dp", "fsdp"), None, None, None),
            P(("dp", "fsdp"), None, None, None),
            P(("dp", "fsdp"), None),
            P(("dp", "fsdp"), None),
            P(),
            P("fsdp", None),
            P(),
            P(),
        ),
        out_specs=(P(("dp", "fsdp")), P("fsdp", None), P("fsdp", None)),
        check_vma=False,
    )
```

```python
import jax
import jax.numpy as jnp
from jax import lax
from jax.experimental import pallas as pl
from jax.experimental.pallas import tpu as pltpu
from jax.sharding import PartitionSpec as P

MODEL = 2560
HEAD = 128
RANK = 64
GROUPS = 16
EPS = 1e-05
BETA = 0.1
ADAPT_SCALE = 0.5

NZ, NX, NY = 8, 4, 4
SHARD = 320
HALF = 160
UNITS = 14
SPLIT_UNITS = 12
SPLITS = SPLIT_UNITS // 3
AHEAD0, AHEAD1, AHEAD2, AHEADZ = 9, 7, 5, 3
BURST = 2
COUNT_UNIT = 12

MESH = pl.DeviceIdType.MESH
F32 = jnp.float32
BF16 = jnp.bfloat16


def mm(a, b):
    return lax.dot_general(a, b, (((1,), (0,)), ((), ())), preferred_element_type=F32)


def mm_nt(a, b):
    return lax.dot_general(a, b, (((1,), (1,)), ((), ())), preferred_element_type=F32)


def kernel(
    len_ref,
    grp_ref,
    gain_ref,
    hid_hbm,
    tgt_hbm,
    w_hbm,
    down_hbm,
    up_t_hbm,
    loss_ref,
    fin_ref,
    wbuf,
    hbuf,
    normed,
    normed_t,
    tbuf,
    down,
    up_t,
    lowq,
    lowv,
    low_t,
    left,
    kbuf,
    k_t,
    vcat,
    mask,
    dvacc,
    dq_all,
    xsum,
    xrecv,
    meta,
    cnt,
    cbuf_p,
    cbuf_z,
    red,
    red2,
    rp,
    rz,
    fin,
    wsem,
    lsem,
    y_send,
    y_recv,
    x_send,
    x_recv,
    z_send,
    z_recv,
    d_send,
    d_recv,
    q_send,
    q_recv,
    c_send,
    c_recv,
    r_send,
    r_recv,
    g_send,
    g_recv,
):
    d = lax.axis_index("dp")
    f = lax.axis_index("fsdp")
    core = d & 1
    xh = (d >> 1) & 1
    z = d >> 2
    par = f & 1
    y = f >> 1
    x = 2 * xh + par

    def dev(zz, xx, yy):
        return (zz * 4 + (xx & 2) + core, yy * 2 + (xx & 1))

    to_y = [dev(z, x, (y + j) & 3) for j in range(NY)]
    to_x = [dev(z, (x + j) & 3, y) for j in range(NX)]
    to_z = [((d + 4 * j) & 31, f) for j in range(NZ)]

    def in_plane(jy, jx):
        return dev(z, (x + jx) & 3, (y + jy) & 3)

    def on_y(j):
        return to_y[j]

    def on_x(j):
        return to_x[j]

    def on_z(j):
        return to_z[j]

    other = 1 - core
    mate = (d + 1 - 2 * core, f)

    def remote(src, dst, send, recv, target):
        return pltpu.make_async_remote_copy(
            src_ref=src,
            dst_ref=dst,
            send_sem=send,
            recv_sem=recv,
            device_id=target,
            device_id_type=MESH,
        )

    own_off = SHARD * f

    y_off = [SHARD * (2 * ((y + j) & 3) + par) for j in range(NY)]
    f_off = [SHARD * ((f + j) & 7) for j in range(8)]

    def shard_off(j):
        return y_off[j]

    def rows(off, n):
        return pl.ds(pl.multiple_of(off, 32), n)

    def column(u):
        h = u // 7
        r = u % 7
        if r == 0:
            return MODEL + HEAD * (2 * core + h)
        if r == 1:
            return MODEL + 4 * HEAD + HEAD * (2 * core + h)
        return HEAD * (10 * core + 5 * h + r - 2)

    def lanes(off, n):
        return pl.ds(pl.multiple_of(off, HEAD), n)

    w_copies = []
    for u in range(UNITS):
        copy = pltpu.make_async_copy(
            w_hbm.at[:, lanes(column(u), HEAD)], wbuf.at[u, rows(own_off, SHARD), :], wsem.at[u]
        )
        copy.start()
        w_copies.append(copy)
        if u == 0:
            hid_copy = pltpu.make_async_copy(hid_hbm, hbuf, lsem.at[0])
            hid_copy.start()
    my_rows = rows(256 * core, 256)
    tgt_copy = pltpu.make_async_copy(
        tgt_hbm.at[:, lanes(1280 * core, 1280)], tbuf.at[my_rows, :], lsem.at[1]
    )
    tgt_copy.start()
    down_copy = pltpu.make_async_copy(down_hbm, down, lsem.at[2])
    down_copy.start()
    up_copy = pltpu.make_async_copy(up_t_hbm, up_t, lsem.at[3])
    up_copy.start()

    barrier = pltpu.get_barrier_semaphore()

    for target in (on_y(1), on_y(3), on_x(1), on_x(3), on_z(1), on_z(7), mate):
        pl.semaphore_signal(barrier, inc=1, device_id=target, device_id_type=MESH)

    lane = lax.broadcasted_iota(jnp.int32, (8, HEAD), 1)
    row = lax.broadcasted_iota(jnp.int32, (8, HEAD), 0)
    meta_own = jnp.where(
        row == 0,
        len_ref[0, 0].astype(F32),
        jnp.where(
            row == 1,
            len_ref[0, 1].astype(F32),
            jnp.where((row == 2) & (lane == grp_ref[0, 0]), F32(1.0), F32(0.0)),
        ),
    )
    meta[pl.ds(core, 1)] = meta_own[None]

    pl.semaphore_wait(barrier, 7)

    def piece(u, off, n):
        return wbuf.at[u, rows(off, n), :]

    def send_y(u, kind, off, n, target):
        ref = piece(u, off, n)
        remote(ref, ref, y_send.at[kind], y_recv.at[kind, u], target).start()

    def send_x(u, off):
        ref = piece(u, off, HALF)
        remote(ref, ref, x_send.at[0], x_recv.at[u], on_x(1)).start()

    def send_x_back(u, off):
        ref = piece(u, off + HALF, HALF)
        remote(ref, ref, x_send.at[1], x_recv.at[u], on_x(3)).start()

    def wait_y(u, kind, n):
        ref = wbuf.at[u, pl.ds(0, n), :]
        remote(ref, ref, y_send.at[kind], y_recv.at[kind, u], on_y(1)).wait_recv()

    z_par = z & 1

    def split(u):
        return (u < SPLIT_UNITS) & (lax.rem(u, 3) < 2)

    def takes(u):
        return split(u) & (lax.rem(u, 3) != z_par)

    def gives(u):
        return split(u) & (lax.rem(u, 3) == z_par)

    def wait_own(u):
        ref = wbuf.at[u, rows(own_off, SHARD), :]
        pltpu.make_async_copy(ref, ref, wsem.at[u]).wait()

    def stage0(u):
        @pl.when(jnp.logical_not(takes(u)))
        def _():
            wait_own(u)
            send_y(u, 0, own_off, SHARD, on_y(1))
            send_y(u, 1, own_off, SHARD, on_y(3))
            send_x(u, own_off)
            send_x_back(u, own_off)

    def stage1(u):
        @pl.when(jnp.logical_not(takes(u)))
        def _():
            wait_y(u, 0, SHARD)
            off = shard_off(3)
            send_y(u, 2, off, HALF, on_y(1))
            send_x(u, off)
            send_x_back(u, off)
            wait_y(u, 1, SHARD)
            off = shard_off(1)
            send_y(u, 3, off + HALF, HALF, on_y(3))
            send_x(u, off)
            send_x_back(u, off)

    def stage2(u):
        @pl.when(jnp.logical_not(takes(u)))
        def _():
            off = shard_off(2)
            wait_y(u, 2, HALF)
            send_x(u, off)
            wait_y(u, 3, HALF)
            send_x_back(u, off)

    def wait_x(u):
        ref = wbuf.at[u, pl.ds(0, 8 * HALF), :]
        remote(ref, ref, x_send.at[0], x_recv.at[u], on_x(1)).wait_recv()

    def send_z(u, way, off, n):
        ref = piece(u, off, n)
        remote(ref, ref, z_send.at[way], z_recv.at[u], on_z((1, NZ - 1)[way])).start()

    def stage_z(u):
        @pl.when(gives(u))
        def _():
            wait_x(u)
            for j in range(1, 8):
                off = f_off[j]
                if j == 4:
                    send_z(u, 0, off, HALF)
                    send_z(u, 1, off + HALF, HALF)
                else:
                    send_z(u, 0 if j < 4 else 1, off, SHARD)

    def stage3(u):
        @pl.when(takes(u))
        def _():
            wait_own(u)
            ref = wbuf.at[u, pl.ds(0, 7 * SHARD), :]
            remote(ref, ref, z_send.at[0], z_recv.at[u], on_z(1)).wait_recv()

        @pl.when(jnp.logical_not(split(u)))
        def _():
            wait_x(u)

    def advance(u):
        for stage, ahead in (
            (stage0, AHEAD0),
            (stage1, AHEAD1),
            (stage2, AHEAD2),
            (stage_z, AHEADZ),
        ):

            @pl.when(u + ahead < UNITS)
            def _(stage=stage, ahead=ahead):
                stage(u + ahead)

        stage3(u)

    def early(tick):
        for stage, ahead in (
            (stage0, AHEAD0),
            (stage1, AHEAD1),
            (stage2, AHEAD2),
            (stage_z, AHEADZ),
        ):
            if 0 <= tick + ahead < UNITS:
                stage(tick + ahead)

    ticks = iter(range(-AHEAD0, 0))
    for _ in range(BURST):
        early(next(ticks))

    meta_copy = remote(meta.at[core], meta.at[core], d_send.at[0], d_recv.at[0], mate)
    meta_copy.start()
    tgt_remote = remote(
        tgt_hbm.at[:, lanes(1280 * other, 1280)],
        tbuf.at[my_rows, :],
        d_send.at[1],
        d_recv.at[1],
        mate,
    )
    tgt_remote.start()

    hid_copy.wait()
    gain = gain_ref[...].reshape(1, MODEL)

    def norm_block(i, carry):
        values = hbuf[pl.ds(pl.multiple_of(32 * i, 32), 32), :].astype(F32)
        power = jnp.mean(values * values, -1, keepdims=True)
        out = (values * lax.rsqrt(power + EPS) * gain).astype(BF16)
        normed[rows(256 * core + 32 * i, 32), :] = out
        return carry

    lax.fori_loop(0, 8, norm_block, 0)
    normed_copy = remote(
        normed.at[my_rows, :], normed.at[my_rows, :], d_send.at[2], d_recv.at[2], mate
    )
    normed_copy.start()
    early(next(ticks))

    meta_copy.wait()
    cnt[0] = meta[0] + meta[1]

    def plane_counts():
        return [
            remote(
                cnt.at[0], cbuf_p.at[j - 1], c_send.at[j - 1], c_recv.at[j - 1], in_plane(j >> 2, j & 3)
            )
            for j in range(1, NX * NY)
        ]

    def z_counts():
        return [
            remote(cnt.at[1], cbuf_z.at[j - 1], c_send.at[14 + j], c_recv.at[14 + j], on_z(j))
            for j in range(1, NZ)
        ]

    def gathered(step, copies, buf):
        for copy in copies:
            copy.wait()
        cnt[step + 1] = cnt[step] + jnp.sum(buf[...], axis=0)

    early(next(ticks))

    key_at = lax.broadcasted_iota(jnp.int32, (HEAD, HEAD), 0)
    query_at = lax.broadcasted_iota(jnp.int32, (HEAD, HEAD), 1)
    for n in range(4):
        length = meta[n // 2, pl.ds(n % 2, 1), :]
        allowed = (key_at <= query_at) & (key_at.astype(F32) < length)
        mask[n] = jnp.where(allowed, F32(1.0), F32(0.0))
    tgt_copy.wait()
    tgt_remote.wait()
    for n in range(4):
        length = meta[n // 2, pl.ds(n % 2, 1), :]
        keep = key_at.astype(F32) < length
        for i in range(10):
            at = (pl.ds(HEAD * n, HEAD), pl.ds(HEAD * i, HEAD))
            tbuf[at] = jnp.where(keep, tbuf[at].astype(F32), F32(0.0)).astype(BF16)
    early(next(ticks))

    down_copy.wait()
    up_copy.wait()
    normed_copy.wait()
    low = mm(normed[...], down[...])
    lowq[...] = low[:, :RANK].astype(BF16)
    lowv[...] = low[:, RANK:].astype(BF16)
    for n in range(4):
        low_t[:, HEAD * n : HEAD * (n + 1)] = (
            low[HEAD * n : HEAD * (n + 1), :].astype(BF16).astype(F32).T
        )
    xsum[...] = jnp.zeros_like(xsum)
    early(next(ticks))
    for tick in ticks:
        early(tick)
    for copy in plane_counts():
        copy.start()

    def head_step(u, h, i):
        advance(u)
        qi = 5 * h + i
        block = 10 * core + qi
        base = mm(normed[...], wbuf[u])
        upq = up_t[:, lanes(HEAD * block, HEAD)]
        qpol = (base + ADAPT_SCALE * mm(lowq[...], upq)).astype(BF16)
        qref = base.astype(BF16)
        for n in range(4):
            at = slice(HEAD * n, HEAD * (n + 1))
            both = jnp.concatenate([qpol[at], qref[at]], 0)
            scores = mm_nt(kbuf[h, at, :], both) * HEAD ** (-0.5)
            allowed = jnp.concatenate([mask[n], mask[n]], 1) > 0.0
            expo = jnp.where(allowed, jnp.exp(scores), F32(0.0))
            probs = expo * (1.0 / jnp.sum(expo, 0, keepdims=True))
            target = tbuf[at, lanes(HEAD * qi, HEAD)]
            d_both = mm_nt(vcat[h, n], target)
            pol = probs[:, :HEAD]
            weighed = pol * d_both[:HEAD]
            token = jnp.sum(weighed, 0, keepdims=True)
            token_ref = jnp.sum(probs[:, HEAD:] * d_both[HEAD:], 0, keepdims=True)
            xsum[HEAD : HEAD + 1, at] += token - token_ref
            d_scores = (weighed - pol * token).astype(BF16)
            dq_all[block, :, at] = mm(k_t[h, :, at], d_scores).astype(BF16)
            dvacc[at, :] += mm(pol.astype(BF16), target)
        remote(dq_all.at[block], dq_all.at[block], q_send.at[qi], q_recv.at[qi], mate).start()
        xsum[0:RANK, :] += mm(upq, dq_all[block])
        for j in range(2):
            at = lanes(HEAD * (2 * qi + j), HEAD)
            normed_t[at, :] = normed[:, at].T

    def group_step(h, carry):
        u = 7 * h
        advance(u)
        keys = mm(normed[...], wbuf[u]).astype(BF16)
        kbuf[h] = keys
        for n in range(4):
            at = slice(HEAD * n, HEAD * (n + 1))
            k_t[h, :, at] = keys[at].astype(F32).T.astype(BF16)
        advance(u + 1)
        base = mm(normed[...], wbuf[u + 1])
        block = 20 + 2 * core + h
        upv = up_t[:, lanes(HEAD * block, HEAD)]
        values = (base + ADAPT_SCALE * mm(lowv[...], upv)).astype(BF16)
        for n in range(4):
            at = slice(HEAD * n, HEAD * (n + 1))
            vcat[h, n, 0:HEAD] = values[at]
            vcat[h, n, HEAD:] = base[at].astype(BF16)
        dvacc[...] = jnp.zeros_like(dvacc)

        def inner(i, inner_carry):
            head_step(u + 2 + i, h, i)

            @pl.when(u + 2 + i == COUNT_UNIT)
            def _():
                gathered(0, plane_counts(), cbuf_p)
                for copy in z_counts():
                    copy.start()

            return inner_carry

        lax.fori_loop(0, 5, inner, 0)
        for n in range(4):
            at = slice(HEAD * n, HEAD * (n + 1))
            dq_all[block, :, at] = dvacc[at, :].T.astype(BF16)
        remote(
            dq_all.at[block], dq_all.at[block], q_send.at[10 + h], q_recv.at[10 + h], mate
        ).start()
        xsum[RANK:HEAD, :] += mm(upv, dq_all[block])
        return carry

    lax.fori_loop(0, 2, group_step, 0)

    x_copy = remote(xsum, xrecv, d_send.at[3], d_recv.at[3], mate)
    x_copy.start()
    gathered(1, z_counts(), cbuf_z)
    weights = []
    for c in range(2):
        count = jnp.sum(cnt[2, 2:3, :] * meta[c, 2:3, :], axis=-1, keepdims=True)
        weights.append(1.0 / (GROUPS * count))
    x_copy.wait()

    differ = xsum[HEAD : HEAD + 1, :] + xrecv[HEAD : HEAD + 1, :]
    diffs = [
        jnp.sum(differ[:, HEAD * n : HEAD * (n + 1)], axis=-1, keepdims=True) * MODEL ** (-0.5)
        for n in range(4)
    ]
    coefs = []
    for c in range(2):
        margin = BETA * (diffs[2 * c] - diffs[2 * c + 1])
        loss = jnp.maximum(-margin, 0.0) + jnp.log1p(jnp.exp(-jnp.abs(margin)))
        slope = -(1.0 / (1.0 + jnp.exp(margin))) * weights[c] * BETA
        slope = slope * (ADAPT_SCALE * MODEL ** (-0.5))
        coefs += [slope, -slope]
        loss_ref[...] = loss if c == 0 else jnp.where(core == 1, loss, loss_ref[...])

    half_row = lax.broadcasted_iota(jnp.int32, (HEAD, 1), 0)
    row_scale = jnp.where(half_row < RANK, F32(HEAD ** (-0.5)), F32(1.0))
    low_parts = []
    for n in range(4):
        at = slice(HEAD * n, HEAD * (n + 1))
        scale = row_scale * coefs[n]
        low_parts.append(((xsum[0:HEAD, at] + xrecv[0:HEAD, at]) * scale).astype(BF16))
        low_t[:, at] = low_t[:, at] * scale
    d_low = jnp.concatenate(low_parts, 1)
    left[0] = low_t[rows(32 * core, 32), :].astype(BF16)
    left[1] = low_t[rows(RANK + 32 * core, 32), :].astype(BF16)

    def mate_blocks(i, carry):
        @pl.when(i < 10)
        def _():
            mine = dq_all.at[10 * core + i]
            remote(mine, mine, q_send.at[i], q_recv.at[i], mate).wait()

        @pl.when(i >= 10)
        def _():
            mine = dq_all.at[20 + 2 * core + i - 10]
            remote(mine, mine, q_send.at[i], q_recv.at[i], mate).wait()

        return carry

    lax.fori_loop(0, 12, mate_blocks, 0)

    copies = []
    for jy in (2, 1, 3, 0):
        yy = (y + jy) & 3
        for jp in (1, 0):
            pp = par ^ jp
            j = 2 * yy + pp
            part = normed_t[rows(SHARD * j + HALF * core, HALF), :]
            red[j, 0:HALF, :] = mm_nt(part, d_low).astype(BF16)
            for i in range(3):
                b = 3 * j + i
                which = (b >= 20).astype(jnp.int32)
                at = HALF + 32 * i
                red[j, at : at + 32, :] = mm_nt(left[which], dq_all[b]).astype(BF16)
            for jx in (jp + 2, jp):
                slot = 4 * jy + jx - 1
                if slot < 0:
                    continue
                xx = (x + jx) & 3
                copy = remote(
                    red.at[j, rows(HEAD * (xx >> 1), HEAD), :],
                    rp.at[slot],
                    r_send.at[slot],
                    r_recv.at[slot],
                    in_plane(jy, jx),
                )
                copy.start()
                copies.append(copy)
    for copy in copies:
        copy.wait()

    total = red[f, rows(HEAD * xh, HEAD), :].astype(F32)
    for j in range(NX * NY - 1):
        total += rp[j].astype(F32)
    red2[...] = total.astype(BF16)

    def z_part(j):
        return red2.at[pl.ds(pl.multiple_of(16 * ((z + j) & 7), 16), 16), :]

    copies = []
    for j in range(1, NZ):
        copy = remote(z_part(j), rz.at[j - 1], r_send.at[14 + j], r_recv.at[14 + j], on_z(j))
        copy.start()
        copies.append(copy)
    for copy in copies:
        copy.wait()
    total = red2[pl.ds(pl.multiple_of(16 * z, 16), 16), :].astype(F32)
    for j in range(NZ - 1):
        total += rz[j].astype(F32)
    mine = pl.ds(pl.multiple_of(HEAD * xh + 16 * z, 16), 16)
    fin[core, mine, :] = total.astype(BF16)

    def hand_out(j, carry):
        ref = fin.at[core, mine, :]
        remote(ref, ref, g_send.at[0], g_recv.at[0], ((d + j) & 31, f)).start()
        return carry

    lax.fori_loop(1, 32, hand_out, 0)
    whole = wbuf.at[0, pl.ds(0, 31 * 16), :]
    remote(whole, whole, g_send.at[0], g_recv.at[0], mate).wait()

    fin_ref[...] = fin[...]

    sent = UNITS - SPLITS
    whole = wbuf.at[pl.ds(0, sent), pl.ds(0, SHARD), :]
    for kind in (0, 1):
        remote(whole, whole, y_send.at[kind], y_recv.at[kind, 0], mate).wait_send()
    whole = wbuf.at[pl.ds(0, sent), pl.ds(0, HALF), :]
    for kind in (2, 3):
        remote(whole, whole, y_send.at[kind], y_recv.at[kind, 0], mate).wait_send()
    whole = wbuf.at[pl.ds(0, sent), pl.ds(0, 4 * HALF), :]
    for kind in (0, 1):
        remote(whole, whole, x_send.at[kind], x_recv.at[0], mate).wait_send()
    whole = wbuf.at[pl.ds(0, SPLITS), pl.ds(0, 7 * HALF), :]
    for way in (0, 1):
        remote(whole, whole, z_send.at[way], z_recv.at[0], mate).wait_send()


def fused(lengths, groups, gain, hidden, targets, weight, adapter_down, adapter_up_t):
    any_spec = pl.BlockSpec(memory_space=pl.ANY)
    smem = pl.BlockSpec(memory_space=pltpu.SMEM)
    vmem = pl.BlockSpec(memory_space=pltpu.VMEM)
    dma = pltpu.SemaphoreType.DMA
    return pl.pallas_call(
        kernel,
        out_shape=(
            jax.ShapeDtypeStruct((1, 1), F32),
            jax.ShapeDtypeStruct((2, 256, HEAD), BF16),
        ),
        in_specs=[smem, smem, vmem, any_spec, any_spec, any_spec, any_spec, any_spec],
        out_specs=(vmem, vmem),
        scratch_shapes=[
            pltpu.VMEM((UNITS, MODEL, HEAD), BF16),
            pltpu.VMEM((256, MODEL), BF16),
            pltpu.VMEM((512, MODEL), BF16),
            pltpu.VMEM((MODEL, 512), BF16),
            pltpu.VMEM((512, 1280), BF16),
            pltpu.VMEM((MODEL, HEAD), BF16),
            pltpu.VMEM((RANK, 3072), BF16),
            pltpu.VMEM((512, RANK), BF16),
            pltpu.VMEM((512, RANK), BF16),
            pltpu.VMEM((HEAD, 512), F32),
            pltpu.VMEM((2, 32, 512), BF16),
            pltpu.VMEM((2, 512, HEAD), BF16),
            pltpu.VMEM((2, HEAD, 512), BF16),
            pltpu.VMEM((2, 4, 256, HEAD), BF16),
            pltpu.VMEM((4, HEAD, HEAD), F32),
            pltpu.VMEM((512, HEAD), F32),
            pltpu.VMEM((24, HEAD, 512), BF16),
            pltpu.VMEM((136, 512), F32),
            pltpu.VMEM((136, 512), F32),
            pltpu.VMEM((2, 8, HEAD), F32),
            pltpu.VMEM((3, 8, HEAD), F32),
            pltpu.VMEM((NX * NY - 1, 8, HEAD), F32),
            pltpu.VMEM((NZ - 1, 8, HEAD), F32),
            pltpu.VMEM((8, 256, HEAD), BF16),
            pltpu.VMEM((HEAD, HEAD), BF16),
            pltpu.VMEM((NX * NY - 1, HEAD, HEAD), BF16),
            pltpu.VMEM((NZ - 1, 16, HEAD), BF16),
            pltpu.VMEM((2, 256, HEAD), BF16),
            dma((UNITS,)),
            dma((4,)),
            dma((4,)),
            dma((4, UNITS)),
            dma((2,)),
            dma((UNITS,)),
            dma((2,)),
            dma((UNITS,)),
            dma((4,)),
            dma((4,)),
            dma((12,)),
            dma((12,)),
            dma((22,)),
            dma((22,)),
            dma((22,)),
            dma((22,)),
            dma((1,)),
            dma((1,)),
        ],
        compiler_params=pltpu.CompilerParams(
            collective_id=0, has_side_effects=True, vmem_limit_bytes=56 * 1024 * 1024
        ),
        cost_estimate=pl.CostEstimate(
            flops=8_000_000_000, bytes_accessed=8_000_000, transcendentals=1_400_000
        ),
    )(lengths, groups, gain, hidden, targets, weight, adapter_down, adapter_up_t)


def finish_kernel(fin_ref, ga_ref, gb_t_ref):
    for c in range(2):
        ga_ref[HALF * c : HALF * (c + 1), :] = fin_ref[c, 0:HALF, :].astype(F32)
        for i in range(3):
            at = HALF + 32 * i
            gb_t_ref[32 * c : 32 * (c + 1), HEAD * i : HEAD * (i + 1)] = fin_ref[
                c, at : at + 32, :
            ].astype(F32)


def finish(fin):
    vmem = pl.BlockSpec(memory_space=pltpu.VMEM)
    return pl.pallas_call(
        finish_kernel,
        out_shape=(
            jax.ShapeDtypeStruct((SHARD, HEAD), F32),
            jax.ShapeDtypeStruct((RANK, 3 * HEAD), F32),
        ),
        in_specs=[vmem],
        out_specs=(vmem, vmem),
    )(fin)


def body(
    hidden,
    targets,
    lengths,
    prompt_group_index,
    input_norm_gain,
    frozen_weight,
    adapter_down,
    adapter_up,
):
    losses, fin = fused(
        lengths,
        prompt_group_index,
        input_norm_gain,
        hidden.reshape(256, MODEL),
        targets.reshape(256, MODEL),
        frozen_weight,
        adapter_down,
        adapter_up.T,
    )
    grad_a, grad_b_t = finish(fin)
    return (losses.reshape(1), grad_a, grad_b_t.T)


def solution(mesh):
    return jax.shard_map(
        body,
        mesh=mesh,
        in_specs=(
            P(("dp", "fsdp"), None, None, None),
            P(("dp", "fsdp"), None, None, None),
            P(("dp", "fsdp"), None),
            P(("dp", "fsdp"), None),
            P(),
            P("fsdp", None),
            P(),
            P(),
        ),
        out_specs=(P(("dp", "fsdp")), P("fsdp", None), P("fsdp", None)),
        check_vma=False,
    )
```

```python
import jax
import jax.numpy as jnp
from jax import lax
from jax.experimental import pallas as pl
from jax.experimental.pallas import tpu as pltpu
from jax.sharding import PartitionSpec as P

MODEL = 2560
HEAD = 128
RANK = 64
GROUPS = 16
EPS = 1e-05
BETA = 0.1
ADAPT_SCALE = 0.5

NZ, NX, NY = 8, 4, 4
SHARD = 320
HALF = 160
UNITS = 14
SPLIT_UNITS = 12
SPLITS = SPLIT_UNITS // 3
AHEAD0, AHEAD1, AHEAD2, AHEADZ = 9, 7, 5, 3
BURST = 2
COUNT_UNIT = 12

MESH = pl.DeviceIdType.MESH
F32 = jnp.float32
BF16 = jnp.bfloat16


def mm(a, b):
    return lax.dot_general(a, b, (((1,), (0,)), ((), ())), preferred_element_type=F32)


def mm_nt(a, b):
    return lax.dot_general(a, b, (((1,), (1,)), ((), ())), preferred_element_type=F32)


def kernel(
    len_ref,
    grp_ref,
    gain_ref,
    hid_hbm,
    tgt_hbm,
    w_hbm,
    down_hbm,
    up_t_hbm,
    loss_ref,
    fin_ref,
    wbuf,
    hbuf,
    normed,
    normed_t,
    tbuf,
    down,
    up_t,
    lowq,
    lowv,
    low_t,
    left,
    kbuf,
    k_t,
    vcat,
    mask,
    dvacc,
    dq_all,
    xsum,
    xrecv,
    meta,
    cnt,
    cbuf_p,
    cbuf_z,
    red,
    red2,
    rp,
    rz,
    fin,
    wsem,
    lsem,
    y_send,
    y_recv,
    x_send,
    x_recv,
    z_send,
    z_recv,
    d_send,
    d_recv,
    q_send,
    q_recv,
    c_send,
    c_recv,
    r_send,
    r_recv,
    g_send,
    g_recv,
):
    d = lax.axis_index("dp")
    f = lax.axis_index("fsdp")
    core = d & 1
    xh = (d >> 1) & 1
    z = d >> 2
    par = f & 1
    y = f >> 1
    x = 2 * xh + par

    def dev(zz, xx, yy):
        return (zz * 4 + (xx & 2) + core, yy * 2 + (xx & 1))

    to_y = [dev(z, x, (y + j) & 3) for j in range(NY)]
    to_x = [dev(z, (x + j) & 3, y) for j in range(NX)]
    to_z = [((d + 4 * j) & 31, f) for j in range(NZ)]

    def in_plane(jy, jx):
        return dev(z, (x + jx) & 3, (y + jy) & 3)

    def on_y(j):
        return to_y[j]

    def on_x(j):
        return to_x[j]

    def on_z(j):
        return to_z[j]

    other = 1 - core
    mate = (d + 1 - 2 * core, f)

    def remote(src, dst, send, recv, target):
        return pltpu.make_async_remote_copy(
            src_ref=src,
            dst_ref=dst,
            send_sem=send,
            recv_sem=recv,
            device_id=target,
            device_id_type=MESH,
        )

    own_off = SHARD * f

    y_off = [SHARD * (2 * ((y + j) & 3) + par) for j in range(NY)]
    f_off = [SHARD * ((f + j) & 7) for j in range(8)]

    def shard_off(j):
        return y_off[j]

    def rows(off, n):
        return pl.ds(pl.multiple_of(off, 32), n)

    def column(u):
        h = u // 7
        r = u % 7
        if r == 0:
            return MODEL + HEAD * (2 * core + h)
        if r == 1:
            return MODEL + 4 * HEAD + HEAD * (2 * core + h)
        return HEAD * (10 * core + 5 * h + r - 2)

    def lanes(off, n):
        return pl.ds(pl.multiple_of(off, HEAD), n)

    w_copies = []
    for u in range(UNITS):
        copy = pltpu.make_async_copy(
            w_hbm.at[:, lanes(column(u), HEAD)], wbuf.at[u, rows(own_off, SHARD), :], wsem.at[u]
        )
        copy.start()
        w_copies.append(copy)
        if u == 0:
            hid_copy = pltpu.make_async_copy(hid_hbm, hbuf, lsem.at[0])
            hid_copy.start()
    my_rows = rows(256 * core, 256)
    tgt_copy = pltpu.make_async_copy(
        tgt_hbm.at[:, lanes(1280 * core, 1280)], tbuf.at[my_rows, :], lsem.at[1]
    )
    tgt_copy.start()
    down_copy = pltpu.make_async_copy(down_hbm, down, lsem.at[2])
    down_copy.start()
    up_copy = pltpu.make_async_copy(up_t_hbm, up_t, lsem.at[3])
    up_copy.start()

    barrier = pltpu.get_barrier_semaphore()

    for target in (on_y(1), on_y(3), on_x(1), on_x(3), on_z(1), on_z(7), mate):
        pl.semaphore_signal(barrier, inc=1, device_id=target, device_id_type=MESH)

    lane = lax.broadcasted_iota(jnp.int32, (8, HEAD), 1)
    row = lax.broadcasted_iota(jnp.int32, (8, HEAD), 0)
    meta_own = jnp.where(
        row == 0,
        len_ref[0, 0].astype(F32),
        jnp.where(
            row == 1,
            len_ref[0, 1].astype(F32),
            jnp.where((row == 2) & (lane == grp_ref[0, 0]), F32(1.0), F32(0.0)),
        ),
    )
    meta[pl.ds(core, 1)] = meta_own[None]

    pl.semaphore_wait(barrier, 7)

    def piece(u, off, n):
        return wbuf.at[u, rows(off, n), :]

    def send_y(u, kind, off, n, target):
        ref = piece(u, off, n)
        remote(ref, ref, y_send.at[kind], y_recv.at[kind, u], target).start()

    def send_x(u, off):
        ref = piece(u, off, HALF)
        remote(ref, ref, x_send.at[0], x_recv.at[u], on_x(1)).start()

    def send_x_back(u, off):
        ref = piece(u, off + HALF, HALF)
        remote(ref, ref, x_send.at[1], x_recv.at[u], on_x(3)).start()

    def wait_y(u, kind, n):
        ref = wbuf.at[u, pl.ds(0, n), :]
        remote(ref, ref, y_send.at[kind], y_recv.at[kind, u], on_y(1)).wait_recv()

    z_par = z & 1

    def split(u):
        return (u < SPLIT_UNITS) & (lax.rem(u, 3) < 2)

    def takes(u):
        return split(u) & (lax.rem(u, 3) != z_par)

    def gives(u):
        return split(u) & (lax.rem(u, 3) == z_par)

    def wait_own(u):
        ref = wbuf.at[u, rows(own_off, SHARD), :]
        pltpu.make_async_copy(ref, ref, wsem.at[u]).wait()

    def stage0(u):
        @pl.when(jnp.logical_not(takes(u)))
        def _():
            wait_own(u)
            send_y(u, 0, own_off, SHARD, on_y(1))
            send_y(u, 1, own_off, SHARD, on_y(3))
            send_x(u, own_off)
            send_x_back(u, own_off)

    def stage1(u):
        @pl.when(jnp.logical_not(takes(u)))
        def _():
            wait_y(u, 0, SHARD)
            off = shard_off(3)
            send_y(u, 2, off, HALF, on_y(1))
            send_x(u, off)
            send_x_back(u, off)
            wait_y(u, 1, SHARD)
            off = shard_off(1)
            send_y(u, 3, off + HALF, HALF, on_y(3))
            send_x(u, off)
            send_x_back(u, off)

    def stage2(u):
        @pl.when(jnp.logical_not(takes(u)))
        def _():
            off = shard_off(2)
            wait_y(u, 2, HALF)
            send_x(u, off)
            wait_y(u, 3, HALF)
            send_x_back(u, off)

    def wait_x(u):
        ref = wbuf.at[u, pl.ds(0, 8 * HALF), :]
        remote(ref, ref, x_send.at[0], x_recv.at[u], on_x(1)).wait_recv()

    def send_z(u, way, off, n):
        ref = piece(u, off, n)
        remote(ref, ref, z_send.at[way], z_recv.at[u], on_z((1, NZ - 1)[way])).start()

    def stage_z(u):
        @pl.when(gives(u))
        def _():
            wait_x(u)
            for j in range(1, 8):
                off = f_off[j]
                if j == 4:
                    send_z(u, 0, off, HALF)
                    send_z(u, 1, off + HALF, HALF)
                else:
                    send_z(u, 0 if j < 4 else 1, off, SHARD)

    def stage3(u):
        @pl.when(takes(u))
        def _():
            wait_own(u)
            ref = wbuf.at[u, pl.ds(0, 7 * SHARD), :]
            remote(ref, ref, z_send.at[0], z_recv.at[u], on_z(1)).wait_recv()

        @pl.when(jnp.logical_not(split(u)))
        def _():
            wait_x(u)

    def advance(u):
        for stage, ahead in (
            (stage0, AHEAD0),
            (stage1, AHEAD1),
            (stage2, AHEAD2),
            (stage_z, AHEADZ),
        ):

            @pl.when(u + ahead < UNITS)
            def _(stage=stage, ahead=ahead):
                stage(u + ahead)

        stage3(u)

    def early(tick):
        for stage, ahead in (
            (stage0, AHEAD0),
            (stage1, AHEAD1),
            (stage2, AHEAD2),
            (stage_z, AHEADZ),
        ):
            if 0 <= tick + ahead < UNITS:
                stage(tick + ahead)

    ticks = iter(range(-AHEAD0, 0))
    for _ in range(BURST):
        early(next(ticks))

    meta_copy = remote(meta.at[core], meta.at[core], d_send.at[0], d_recv.at[0], mate)
    meta_copy.start()
    tgt_remote = remote(
        tgt_hbm.at[:, lanes(1280 * other, 1280)],
        tbuf.at[my_rows, :],
        d_send.at[1],
        d_recv.at[1],
        mate,
    )
    tgt_remote.start()

    hid_copy.wait()
    gain = gain_ref[...].reshape(1, MODEL)

    def norm_block(i, carry):
        values = hbuf[pl.ds(pl.multiple_of(32 * i, 32), 32), :].astype(F32)
        power = jnp.mean(values * values, -1, keepdims=True)
        out = (values * lax.rsqrt(power + EPS) * gain).astype(BF16)
        normed[rows(256 * core + 32 * i, 32), :] = out
        return carry

    lax.fori_loop(0, 8, norm_block, 0)
    normed_copy = remote(
        normed.at[my_rows, :], normed.at[my_rows, :], d_send.at[2], d_recv.at[2], mate
    )
    normed_copy.start()
    early(next(ticks))

    meta_copy.wait()
    cnt[0] = meta[0] + meta[1]

    def plane_counts():
        return [
            remote(
                cnt.at[0], cbuf_p.at[j - 1], c_send.at[j - 1], c_recv.at[j - 1], in_plane(j >> 2, j & 3)
            )
            for j in range(1, NX * NY)
        ]

    def z_counts():
        return [
            remote(cnt.at[1], cbuf_z.at[j - 1], c_send.at[14 + j], c_recv.at[14 + j], on_z(j))
            for j in range(1, NZ)
        ]

    def gathered(step, copies, buf):
        for copy in copies:
            copy.wait()
        cnt[step + 1] = cnt[step] + jnp.sum(buf[...], axis=0)

    early(next(ticks))

    key_at = lax.broadcasted_iota(jnp.int32, (HEAD, HEAD), 0)
    query_at = lax.broadcasted_iota(jnp.int32, (HEAD, HEAD), 1)
    for n in range(4):
        length = meta[n // 2, pl.ds(n % 2, 1), :]
        allowed = (key_at <= query_at) & (key_at.astype(F32) < length)
        mask[n] = jnp.where(allowed, F32(1.0), F32(0.0))
    tgt_copy.wait()
    tgt_remote.wait()
    for n in range(4):
        length = meta[n // 2, pl.ds(n % 2, 1), :]
        keep = key_at.astype(F32) < length
        for i in range(10):
            at = (pl.ds(HEAD * n, HEAD), pl.ds(HEAD * i, HEAD))
            tbuf[at] = jnp.where(keep, tbuf[at].astype(F32), F32(0.0)).astype(BF16)
    early(next(ticks))

    down_copy.wait()
    up_copy.wait()
    normed_copy.wait()
    low = mm(normed[...], down[...])
    lowq[...] = low[:, :RANK].astype(BF16)
    lowv[...] = low[:, RANK:].astype(BF16)
    for n in range(4):
        low_t[:, HEAD * n : HEAD * (n + 1)] = (
            low[HEAD * n : HEAD * (n + 1), :].astype(BF16).astype(F32).T
        )
    xsum[...] = jnp.zeros_like(xsum)
    early(next(ticks))
    for tick in ticks:
        early(tick)
    for copy in plane_counts():
        copy.start()

    def head_step(u, h, i):
        advance(u)
        qi = 5 * h + i
        block = 10 * core + qi
        base = mm(normed[...], wbuf[u])
        upq = up_t[:, lanes(HEAD * block, HEAD)]
        qpol = (base + ADAPT_SCALE * mm(lowq[...], upq)).astype(BF16)
        qref = base.astype(BF16)
        for n in range(4):
            at = slice(HEAD * n, HEAD * (n + 1))
            both = jnp.concatenate([qpol[at], qref[at]], 0)
            scores = mm_nt(kbuf[h, at, :], both) * HEAD ** (-0.5)
            allowed = jnp.concatenate([mask[n], mask[n]], 1) > 0.0
            expo = jnp.where(allowed, jnp.exp(scores), F32(0.0))
            probs = expo * (1.0 / jnp.sum(expo, 0, keepdims=True))
            target = tbuf[at, lanes(HEAD * qi, HEAD)]
            d_both = mm_nt(vcat[h, n], target)
            pol = probs[:, :HEAD]
            weighed = pol * d_both[:HEAD]
            token = jnp.sum(weighed, 0, keepdims=True)
            token_ref = jnp.sum(probs[:, HEAD:] * d_both[HEAD:], 0, keepdims=True)
            xsum[HEAD : HEAD + 1, at] += token - token_ref
            d_scores = (weighed - pol * token).astype(BF16)
            dq_all[block, :, at] = mm(k_t[h, :, at], d_scores).astype(BF16)
            dvacc[at, :] += mm(pol.astype(BF16), target)
        remote(dq_all.at[block], dq_all.at[block], q_send.at[qi], q_recv.at[qi], mate).start()
        xsum[0:RANK, :] += mm(upq, dq_all[block])
        for j in range(2):
            at = lanes(HEAD * (2 * qi + j), HEAD)
            normed_t[at, :] = normed[:, at].T

    def group_step(h, carry):
        u = 7 * h
        advance(u)
        keys = mm(normed[...], wbuf[u]).astype(BF16)
        kbuf[h] = keys
        for n in range(4):
            at = slice(HEAD * n, HEAD * (n + 1))
            k_t[h, :, at] = keys[at].astype(F32).T.astype(BF16)
        advance(u + 1)
        base = mm(normed[...], wbuf[u + 1])
        block = 20 + 2 * core + h
        upv = up_t[:, lanes(HEAD * block, HEAD)]
        values = (base + ADAPT_SCALE * mm(lowv[...], upv)).astype(BF16)
        for n in range(4):
            at = slice(HEAD * n, HEAD * (n + 1))
            vcat[h, n, 0:HEAD] = values[at]
            vcat[h, n, HEAD:] = base[at].astype(BF16)
        dvacc[...] = jnp.zeros_like(dvacc)

        def inner(i, inner_carry):
            head_step(u + 2 + i, h, i)

            @pl.when(u + 2 + i == COUNT_UNIT)
            def _():
                gathered(0, plane_counts(), cbuf_p)
                for copy in z_counts():
                    copy.start()

            return inner_carry

        lax.fori_loop(0, 5, inner, 0)
        for n in range(4):
            at = slice(HEAD * n, HEAD * (n + 1))
            dq_all[block, :, at] = dvacc[at, :].T.astype(BF16)
        remote(
            dq_all.at[block], dq_all.at[block], q_send.at[10 + h], q_recv.at[10 + h], mate
        ).start()
        xsum[RANK:HEAD, :] += mm(upv, dq_all[block])
        return carry

    lax.fori_loop(0, 2, group_step, 0)

    x_copy = remote(xsum, xrecv, d_send.at[3], d_recv.at[3], mate)
    x_copy.start()
    gathered(1, z_counts(), cbuf_z)
    weights = []
    for c in range(2):
        count = jnp.sum(cnt[2, 2:3, :] * meta[c, 2:3, :], axis=-1, keepdims=True)
        weights.append(1.0 / (GROUPS * count))
    x_copy.wait()

    differ = xsum[HEAD : HEAD + 1, :] + xrecv[HEAD : HEAD + 1, :]
    diffs = [
        jnp.sum(differ[:, HEAD * n : HEAD * (n + 1)], axis=-1, keepdims=True) * MODEL ** (-0.5)
        for n in range(4)
    ]
    coefs = []
    for c in range(2):
        margin = BETA * (diffs[2 * c] - diffs[2 * c + 1])
        loss = jnp.maximum(-margin, 0.0) + jnp.log1p(jnp.exp(-jnp.abs(margin)))
        slope = -(1.0 / (1.0 + jnp.exp(margin))) * weights[c] * BETA
        slope = slope * (ADAPT_SCALE * MODEL ** (-0.5))
        coefs += [slope, -slope]
        loss_ref[...] = loss if c == 0 else jnp.where(core == 1, loss, loss_ref[...])

    half_row = lax.broadcasted_iota(jnp.int32, (HEAD, 1), 0)
    row_scale = jnp.where(half_row < RANK, F32(HEAD ** (-0.5)), F32(1.0))
    low_parts = []
    for n in range(4):
        at = slice(HEAD * n, HEAD * (n + 1))
        scale = row_scale * coefs[n]
        low_parts.append(((xsum[0:HEAD, at] + xrecv[0:HEAD, at]) * scale).astype(BF16))
        low_t[:, at] = low_t[:, at] * scale
    d_low = jnp.concatenate(low_parts, 1)
    left[0] = low_t[rows(32 * core, 32), :].astype(BF16)
    left[1] = low_t[rows(RANK + 32 * core, 32), :].astype(BF16)

    def mate_blocks(i, carry):
        @pl.when(i < 10)
        def _():
            mine = dq_all.at[10 * core + i]
            remote(mine, mine, q_send.at[i], q_recv.at[i], mate).wait()

        @pl.when(i >= 10)
        def _():
            mine = dq_all.at[20 + 2 * core + i - 10]
            remote(mine, mine, q_send.at[i], q_recv.at[i], mate).wait()

        return carry

    lax.fori_loop(0, 12, mate_blocks, 0)

    copies = []
    for jy in (2, 1, 3, 0):
        yy = (y + jy) & 3
        for jp in (1, 0):
            pp = par ^ jp
            j = 2 * yy + pp
            part = normed_t[rows(SHARD * j + HALF * core, HALF), :]
            red[j, 0:HALF, :] = mm_nt(part, d_low).astype(BF16)
            for i in range(3):
                b = 3 * j + i
                which = (b >= 20).astype(jnp.int32)
                at = HALF + 32 * i
                red[j, at : at + 32, :] = mm_nt(left[which], dq_all[b]).astype(BF16)
            for jx in (jp + 2, jp):
                slot = 4 * jy + jx - 1
                if slot < 0:
                    continue
                xx = (x + jx) & 3
                copy = remote(
                    red.at[j, rows(HEAD * (xx >> 1), HEAD), :],
                    rp.at[slot],
                    r_send.at[slot],
                    r_recv.at[slot],
                    in_plane(jy, jx),
                )
                copy.start()
                copies.append(copy)
    for copy in copies:
        copy.wait()

    total = red[f, rows(HEAD * xh, HEAD), :].astype(F32)
    for j in range(NX * NY - 1):
        total += rp[j].astype(F32)
    red2[...] = total.astype(BF16)

    def z_part(j):
        return red2.at[pl.ds(pl.multiple_of(16 * ((z + j) & 7), 16), 16), :]

    copies = []
    for j in (4, 3, 5, 2, 6, 1, 7):
        copy = remote(z_part(j), rz.at[j - 1], r_send.at[14 + j], r_recv.at[14 + j], on_z(j))
        copy.start()
        copies.append(copy)
    for copy in copies:
        copy.wait()
    total = red2[pl.ds(pl.multiple_of(16 * z, 16), 16), :].astype(F32)
    for j in range(NZ - 1):
        total += rz[j].astype(F32)
    mine = pl.ds(pl.multiple_of(HEAD * xh + 16 * z, 16), 16)
    fin[core, mine, :] = total.astype(BF16)

    final = fin.at[core, mine, :]
    for j in sorted(range(1, 32), key=lambda j: abs(j - 16)):
        remote(final, final, g_send.at[0], g_recv.at[0], ((d + j) & 31, f)).start()
    whole = wbuf.at[0, pl.ds(0, 31 * 16), :]
    remote(whole, whole, g_send.at[0], g_recv.at[0], mate).wait()

    fin_ref[...] = fin[...]

    sent = UNITS - SPLITS
    whole = wbuf.at[pl.ds(0, sent), pl.ds(0, SHARD), :]
    for kind in (0, 1):
        remote(whole, whole, y_send.at[kind], y_recv.at[kind, 0], mate).wait_send()
    whole = wbuf.at[pl.ds(0, sent), pl.ds(0, HALF), :]
    for kind in (2, 3):
        remote(whole, whole, y_send.at[kind], y_recv.at[kind, 0], mate).wait_send()
    whole = wbuf.at[pl.ds(0, sent), pl.ds(0, 4 * HALF), :]
    for kind in (0, 1):
        remote(whole, whole, x_send.at[kind], x_recv.at[0], mate).wait_send()
    whole = wbuf.at[pl.ds(0, SPLITS), pl.ds(0, 7 * HALF), :]
    for way in (0, 1):
        remote(whole, whole, z_send.at[way], z_recv.at[0], mate).wait_send()


def fused(lengths, groups, gain, hidden, targets, weight, adapter_down, adapter_up_t):
    any_spec = pl.BlockSpec(memory_space=pl.ANY)
    smem = pl.BlockSpec(memory_space=pltpu.SMEM)
    vmem = pl.BlockSpec(memory_space=pltpu.VMEM)
    dma = pltpu.SemaphoreType.DMA
    return pl.pallas_call(
        kernel,
        out_shape=(
            jax.ShapeDtypeStruct((1, 1), F32),
            jax.ShapeDtypeStruct((2, 256, HEAD), BF16),
        ),
        in_specs=[smem, smem, vmem, any_spec, any_spec, any_spec, any_spec, any_spec],
        out_specs=(vmem, vmem),
        scratch_shapes=[
            pltpu.VMEM((UNITS, MODEL, HEAD), BF16),
            pltpu.VMEM((256, MODEL), BF16),
            pltpu.VMEM((512, MODEL), BF16),
            pltpu.VMEM((MODEL, 512), BF16),
            pltpu.VMEM((512, 1280), BF16),
            pltpu.VMEM((MODEL, HEAD), BF16),
            pltpu.VMEM((RANK, 3072), BF16),
            pltpu.VMEM((512, RANK), BF16),
            pltpu.VMEM((512, RANK), BF16),
            pltpu.VMEM((HEAD, 512), F32),
            pltpu.VMEM((2, 32, 512), BF16),
            pltpu.VMEM((2, 512, HEAD), BF16),
            pltpu.VMEM((2, HEAD, 512), BF16),
            pltpu.VMEM((2, 4, 256, HEAD), BF16),
            pltpu.VMEM((4, HEAD, HEAD), F32),
            pltpu.VMEM((512, HEAD), F32),
            pltpu.VMEM((24, HEAD, 512), BF16),
            pltpu.VMEM((136, 512), F32),
            pltpu.VMEM((136, 512), F32),
            pltpu.VMEM((2, 8, HEAD), F32),
            pltpu.VMEM((3, 8, HEAD), F32),
            pltpu.VMEM((NX * NY - 1, 8, HEAD), F32),
            pltpu.VMEM((NZ - 1, 8, HEAD), F32),
            pltpu.VMEM((8, 256, HEAD), BF16),
            pltpu.VMEM((HEAD, HEAD), BF16),
            pltpu.VMEM((NX * NY - 1, HEAD, HEAD), BF16),
            pltpu.VMEM((NZ - 1, 16, HEAD), BF16),
            pltpu.VMEM((2, 256, HEAD), BF16),
            dma((UNITS,)),
            dma((4,)),
            dma((4,)),
            dma((4, UNITS)),
            dma((2,)),
            dma((UNITS,)),
            dma((2,)),
            dma((UNITS,)),
            dma((4,)),
            dma((4,)),
            dma((12,)),
            dma((12,)),
            dma((22,)),
            dma((22,)),
            dma((22,)),
            dma((22,)),
            dma((1,)),
            dma((1,)),
        ],
        compiler_params=pltpu.CompilerParams(
            collective_id=0, has_side_effects=True, vmem_limit_bytes=56 * 1024 * 1024
        ),
        cost_estimate=pl.CostEstimate(
            flops=8_000_000_000, bytes_accessed=8_000_000, transcendentals=1_400_000
        ),
    )(lengths, groups, gain, hidden, targets, weight, adapter_down, adapter_up_t)


def finish_kernel(fin_ref, ga_ref, gb_t_ref):
    for c in range(2):
        ga_ref[HALF * c : HALF * (c + 1), :] = fin_ref[c, 0:HALF, :].astype(F32)
        for i in range(3):
            at = HALF + 32 * i
            gb_t_ref[32 * c : 32 * (c + 1), HEAD * i : HEAD * (i + 1)] = fin_ref[
                c, at : at + 32, :
            ].astype(F32)


def finish(fin):
    vmem = pl.BlockSpec(memory_space=pltpu.VMEM)
    return pl.pallas_call(
        finish_kernel,
        out_shape=(
            jax.ShapeDtypeStruct((SHARD, HEAD), F32),
            jax.ShapeDtypeStruct((RANK, 3 * HEAD), F32),
        ),
        in_specs=[vmem],
        out_specs=(vmem, vmem),
    )(fin)


def body(
    hidden,
    targets,
    lengths,
    prompt_group_index,
    input_norm_gain,
    frozen_weight,
    adapter_down,
    adapter_up,
):
    losses, fin = fused(
        lengths,
        prompt_group_index,
        input_norm_gain,
        hidden.reshape(256, MODEL),
        targets.reshape(256, MODEL),
        frozen_weight,
        adapter_down,
        adapter_up.T,
    )
    grad_a, grad_b_t = finish(fin)
    return (losses.reshape(1), grad_a, grad_b_t.T)


def solution(mesh):
    return jax.shard_map(
        body,
        mesh=mesh,
        in_specs=(
            P(("dp", "fsdp"), None, None, None),
            P(("dp", "fsdp"), None, None, None),
            P(("dp", "fsdp"), None),
            P(("dp", "fsdp"), None),
            P(),
            P("fsdp", None),
            P(),
            P(),
        ),
        out_specs=(P(("dp", "fsdp")), P("fsdp", None), P("fsdp", None)),
        check_vma=False,
    )
```
